512 devices in a mesh: gx: 32 (over x, y), gy: 16 (over z, core).
Axes of the slice: x: 4, y: 8, z: 8, core: 2. Of those that a mesh axis runs over, the one named last changes fastest.
Arguments:
- orbitals: bfloat16 [32, 16, 1, 64, 4096], P('gx', 'gy'), may hold values from -6 to 6
- pair_table: int32 [32, 16, 4, 5], P('gx', 'gy'), may hold values from -32 to 511, as said below
Outputs:
- exchange_terms: float32 [32, 16, 1, 64, 4096], P('gx', 'gy')
The draws below stay inside these ranges and needn't reach their ends.
Inputs may be any that keep to these rules, and one draw needn't show every extreme that they name: `pair_table`: each device's list holds its live rows first, then empty rows (-1, -1, 0, 0, 0); some device lists exactly 4 live rows. In a live row, orbital i belongs to the listing device; orbital j != i belongs to that device or to one of the eight devices around it in the two axes, wrapping around both axes. Each unordered pair of orbitals is listed at most once overall. Every component of s lies between -32 and 32.
All inputs are finite; a program needn't handle non-finite values.
Results may differ from the reference program's by a relative error of at most 0.00035.
Values may be sent and summed in bfloat16 or wider, within the bound.
A program may use at most 128 MiB of HBM per device.

```python
import math
import jax
import jax.numpy as jnp
import numpy as np
from jax import lax

B = 64
ORB_DEV = 1
MOST = 4
N_GX = 32
N_GY = 16


def draw_pair_table(key, part):
    key = jax.random.fold_in(key, 7)
    keys = jax.random.split(key, 5)
    candidates = []
    for first_slot in range(ORB_DEV):
        for second_slot in range(ORB_DEV):
            for step_x, step_y in ((0, 1), (1, -1), (1, 0), (1, 1)):
                candidates.append((first_slot, second_slot, step_x, step_y))
        for second_slot in range(first_slot + 1, ORB_DEV):
            candidates.append((first_slot, second_slot, 0, 0))
    cand_table = jnp.asarray(np.array(candidates, np.int32))
    cand_total = len(candidates)
    devices = N_GX * N_GY
    device_ids = jnp.arange(devices, dtype=jnp.int32)
    place_x = device_ids // N_GY
    place_y = device_ids % N_GY
    move_x = cand_table[:, 2]
    move_y = cand_table[:, 3]
    target = (place_x[:, None] + move_x[None, :]) % N_GX * N_GY + (place_y[:, None] + move_y[None, :]) % N_GY
    source = (place_x[:, None] - move_x[None, :]) % N_GX * N_GY + (place_y[:, None] - move_y[None, :]) % N_GY
    same_device = (move_x == 0) & (move_y == 0)
    busiest = jax.random.randint(keys[2], (), 0, devices)
    coins = jax.random.randint(keys[0], (devices, cand_total), 0, 2)
    coins = jnp.where(target == busiest, 1, coins)
    coins = jnp.where(device_ids[:, None] == busiest, 0, coins)
    coins = jnp.where(same_device[None, :], 0, coins)
    offsets = jax.random.randint(keys[3], (devices, cand_total, 3), -(B // 2), B // 2 + 1)
    forward_first = device_ids[:, None] * ORB_DEV + cand_table[None, :, 0]
    forward_second = target * ORB_DEV + cand_table[None, :, 1]
    forward_rows = jnp.concatenate([forward_first[..., None], forward_second[..., None], offsets], axis=-1)
    forward_ok = coins == 0
    cand_index = jnp.arange(cand_total, dtype=jnp.int32)[None, :]
    backward_ok = coins[source, cand_index] == 1
    backward_first = device_ids[:, None] * ORB_DEV + cand_table[None, :, 1]
    backward_second = source * ORB_DEV + cand_table[None, :, 0]
    backward_offsets = -offsets[source, cand_index]
    backward_rows = jnp.concatenate([backward_first[..., None], backward_second[..., None], backward_offsets], axis=-1)
    pool_rows = jnp.concatenate([forward_rows, backward_rows], axis=1).astype(jnp.int32)
    pool_ok = jnp.concatenate([forward_ok, backward_ok], axis=1)
    pool_size = 2 * cand_total
    scores = jax.random.randint(keys[1], (devices, pool_size), 0, 65536) * pool_size + jnp.arange(pool_size, dtype=jnp.int32)[None, :]
    scores = jnp.where(pool_ok, scores, scores + 1073741824)
    chosen = jnp.argsort(scores, axis=1, stable=True)[:, :MOST]
    picked = jnp.take_along_axis(pool_rows, chosen[..., None], axis=1)
    available = jnp.sum(pool_ok.astype(jnp.int32), axis=1)
    live_counts = jnp.minimum(jax.random.randint(keys[4], (devices,), 0, MOST + 1), available)
    live_counts = jnp.where(device_ids == busiest, MOST, live_counts)
    is_live = jnp.arange(MOST)[None, :] < live_counts[:, None]
    empty_row = jnp.array([-1, -1, 0, 0, 0], jnp.int32)
    filled = jnp.where(is_live[..., None], picked, empty_row)
    return filled.astype(jnp.int32).reshape(N_GX, N_GY, MOST, 5)


def levels(own_key, dims, pieces, smallest, largest):
    def one(position, parts):
        heights = jax.random.uniform(jax.random.fold_in(jax.random.fold_in(own_key, 6), position), (parts,), jnp.float32, smallest / len(pieces), largest / len(pieces))
        return jnp.repeat(jnp.exp(heights), dims[position] // parts).reshape((-1,) + (1,) * (len(dims) - position - 1))

    gain = one(*pieces[0])
    for cut in pieces[1:]:
        gain = gain * one(*cut)
    return gain


def scatter_about(own_key, dims, spread, most, cuts=(), kind=jnp.bfloat16):
    values = spread * jax.random.normal(own_key, dims, jnp.float32)
    if cuts:
        values = values * levels(own_key, dims, cuts, -0.22, 0.18)
    return jnp.clip(values, -most, most).astype(kind)


def setup_inputs(seed: int = 0) -> dict:
    arg_keys = jax.random.split(jax.random.key(seed), 3)
    return {
        "orbitals": scatter_about(arg_keys[0], (N_GX, N_GY, ORB_DEV, B, B * B), 1.0, 6.0, ((0, 32), (1, 16))),
        "pair_table": draw_pair_table(jax.random.fold_in(arg_keys[2], 71), 0),
    }


HIGH = lax.Precision.HIGHEST


def make_sine(box_len):
    positions = jnp.arange(box_len, dtype=jnp.float32) + 1.0
    return jnp.sin(math.pi * positions[:, None] * positions[None, :] / (box_len + 1))


def inverse_weights(box_len):
    positions = jnp.arange(box_len, dtype=jnp.float32) + 1.0
    eigen_vals = 2.0 - 2.0 * jnp.cos(math.pi * positions / (box_len + 1))
    denominator = eigen_vals[:, None, None] + eigen_vals[None, :, None] + eigen_vals[None, None, :]
    return (2.0 / (box_len + 1)) ** 3 / denominator


def transform(grid_field, sine_table):
    box_len = grid_field.shape[0]
    result = jnp.dot(sine_table, grid_field.reshape(box_len, box_len * box_len), precision=HIGH)
    result = result.reshape(box_len, box_len, box_len)
    result = jnp.einsum("kn,anb->akb", sine_table, result, precision=HIGH)
    return jnp.einsum("kn,abn->abk", sine_table, result, precision=HIGH)


def move_in(box_data, offset_cells):
    half_box = box_data.shape[0] // 2
    padded = jnp.pad(box_data, half_box)
    corner = (half_box - offset_cells).astype(jnp.int32)
    return lax.dynamic_slice(padded, (corner[0], corner[1], corner[2]), box_data.shape)


def move_out(grid_field, offset_cells):
    half_box = grid_field.shape[0] // 2
    padded = jnp.pad(grid_field, half_box)
    corner = (half_box + offset_cells).astype(jnp.int32)
    return lax.dynamic_slice(padded, (corner[0], corner[1], corner[2]), grid_field.shape)


def pair_terms(first_box, second_box, offset_cells, sine_table, weights):
    partner = move_in(second_box, offset_cells).astype(jnp.float32)
    own_values = first_box.astype(jnp.float32)
    density = own_values * partner
    potential = transform(transform(density, sine_table) * weights, sine_table)
    return -potential * partner, move_out(-potential * own_values, offset_cells)


def reference(orbitals, pair_table):
    box_len = orbitals.shape[3]
    box_stack = orbitals.reshape(-1, box_len, box_len, box_len)
    pair_rows = pair_table.reshape(-1, 5)
    sine_table = make_sine(box_len)
    weights = inverse_weights(box_len)

    def add_pair(running, pair_row):
        def live_pair(current):
            first_slot = jnp.maximum(pair_row[0], 0)
            second_slot = jnp.maximum(pair_row[1], 0)
            own_term, partner_term = pair_terms(box_stack[first_slot], box_stack[second_slot], pair_row[2:5], sine_table, weights)
            return current.at[first_slot].add(own_term).at[second_slot].add(partner_term)

        return lax.cond(pair_row[0] >= 0, live_pair, lambda kept: kept, running), None

    exchange_sum, unused = lax.scan(add_pair, jnp.zeros(box_stack.shape, jnp.float32), pair_rows)
    return exchange_sum.reshape(orbitals.shape)
```

```python
import math

import jax
import jax.numpy as jnp
import numpy as np
from jax import lax
from jax.experimental import pallas as pl
from jax.experimental.pallas import tpu as pltpu
from jax.sharding import PartitionSpec as P

MESH = pl.DeviceIdType.MESH
F32 = jnp.float32
BF16 = jnp.bfloat16
BOX = 64
LANES = 128
CHUNKS = BOX * BOX // LANES
PAD = 17
ROWS = CHUNKS * BOX
EDGES = 4


def tables():
    cells = np.arange(BOX, dtype=np.float64) + 1
    sine = np.sin(math.pi * cells[:, None] * cells[None, :] / (BOX + 1))
    high = sine.astype(BF16)
    low = (sine - high.astype(np.float64)).astype(BF16)
    none = np.zeros_like(high)
    both = lambda part: np.block([[part, none], [none, part]])
    left = np.concatenate([high, high, low], axis=1)
    right = np.block([[both(high), both(low)], [both(high), both(none)]])
    eigen = 2 - 2 * np.cos(math.pi * cells / (BOX + 1))
    half = np.arange(BOX // 2)[:, None, None]
    middle = np.arange(BOX)[None, :, None]
    lane = np.arange(LANES)[None, None, :]
    total = eigen[lane // BOX * (BOX // 2) + half] + eigen[middle] + eigen[lane % BOX]
    weight = (2 / (BOX + 1)) ** 3 / total
    return left, right, weight.reshape(ROWS, LANES).astype(np.float32)


def split(values):
    high = values.astype(BF16)
    return high, (values - high.astype(F32)).astype(BF16)


def shift_matrix(amount, offset):
    row = lax.broadcasted_iota(jnp.int32, (2 * LANES, LANES), 0)
    col = lax.broadcasted_iota(jnp.int32, (2 * LANES, LANES), 1)
    cell = (col & (BOX - 1)) - offset
    inside = (row == col + amount) & (cell >= 0) & (cell < BOX)
    return jnp.where(inside, 1.0, 0.0).astype(BF16)


def rows_dot(left, values):
    high, low = split(values)
    return jnp.dot(left, jnp.concatenate([high, low, high], axis=0), preferred_element_type=F32)


def lanes_dot(values, right):
    high, low = split(values)
    both = jnp.dot(jnp.concatenate([high, low], axis=1), right, preferred_element_type=F32)
    return both[:, :LANES] + both[:, LANES:]


def beside(chunks):
    before = chunks[:-1].reshape(ROWS, LANES)
    return jnp.concatenate([before, chunks[1:].reshape(ROWS, LANES)], axis=1)


def kernel(
    orb_ref, tab_ref, left_ref, right_ref, weight_ref, out_ref,
    own, near, near_tab, tab_here, tab_near,
    padded, shifted, partner, first, first_term, field, total,
    coded, scales, got, got_scales,
    box_send, box_recv, tab_send, tab_recv, term_send, term_recv, scale_send, scale_recv, local_sem,
):
    span_x, span_y = lax.axis_size("gx"), lax.axis_size("gy")
    here_x, here_y = lax.axis_index("gx"), lax.axis_index("gy")
    sign = 1 - 2 * lax.rem(here_y, 2)

    def at(step_x, step_y):
        return (lax.rem(here_x + step_x + span_x, span_x), lax.rem(here_y + step_y + span_y, span_y))

    targets = [at(0, 1), at(sign, 0), at(1, 1), at(-1, 1)]
    users = [at(0, -1), at(-sign, 0), at(-1, -1), at(1, -1)]

    def pick(options, edge):
        chosen = options[0]
        for number in range(1, EDGES):
            chosen = tuple(jnp.where(edge == number, new, old) for new, old in zip(options[number], chosen))
        return chosen

    barrier = pltpu.get_barrier_semaphore()
    for device in targets + users:
        pl.semaphore_signal(barrier, inc=1, device_id=device, device_id_type=MESH)
    for chunk in range(CHUNKS):
        own[chunk] = orb_ref[:, chunk * LANES:(chunk + 1) * LANES]
    pl.semaphore_wait(barrier, 2 * EDGES)

    def tab_copy(edge, device):
        return pltpu.make_async_remote_copy(
            src_ref=tab_ref, dst_ref=near_tab.at[edge], send_sem=tab_send.at[edge],
            recv_sem=tab_recv.at[edge], device_id=device, device_id_type=MESH)

    def box_copy(edge, device):
        return pltpu.make_async_remote_copy(
            src_ref=own, dst_ref=near.at[edge], send_sem=box_send.at[edge],
            recv_sem=box_recv.at[edge], device_id=device, device_id_type=MESH)

    def term_copy(edge, device):
        return pltpu.make_async_remote_copy(
            src_ref=coded.at[edge], dst_ref=got.at[edge], send_sem=term_send.at[edge],
            recv_sem=term_recv.at[edge], device_id=device, device_id_type=MESH)

    def scale_copy(edge, device):
        return pltpu.make_async_remote_copy(
            src_ref=scales.at[edge], dst_ref=got_scales.at[edge], send_sem=scale_send.at[edge],
            recv_sem=scale_recv.at[edge], device_id=device, device_id_type=MESH)

    for edge in range(EDGES):
        tab_copy(edge, users[edge]).start()
        box_copy(edge, users[edge]).start()

    local = pltpu.make_async_copy(tab_ref, tab_here, local_sem)
    local.start()
    padded[...] = jnp.zeros_like(padded)
    shifted[...] = jnp.zeros_like(shifted)
    total[...] = jnp.zeros_like(total)
    local.wait()

    left = left_ref[...]
    low = lax.broadcasted_iota(jnp.int32, (BOX // 2, LANES), 1) < BOX
    me = here_x * span_y + here_y

    def pair(edge, carry):
        target = pick(targets, edge)
        other = target[0] * span_y + target[1]
        tab_copy(edge, target).wait_recv()
        copy = pltpu.make_async_copy(near_tab.at[edge], tab_near, local_sem)
        copy.start()
        copy.wait()
        listed = jnp.int32(0)
        wanted = jnp.int32(0)
        offset = [jnp.int32(0)] * 3
        for row in range(EDGES):
            mine = (tab_here[row, 0] == me) & (tab_here[row, 1] == other)
            theirs = (tab_near[row, 0] == other) & (tab_near[row, 1] == me)
            listed = jnp.where(mine, 1, listed)
            wanted = jnp.where(theirs, 1, wanted)
            for dim in range(3):
                value = jnp.where(theirs, tab_near[row, 2 + dim], offset[dim])
                offset[dim] = jnp.where(mine, tab_here[row, 2 + dim], value)
        is_mine = listed == 1
        is_live = (listed + wanted) > 0
        box_copy(edge, target).wait_recv()

        ours = own[...].astype(F32)
        theirs = near[edge].astype(F32)
        chosen = jnp.where(is_mine, ours, theirs)
        first[...] = jnp.where(is_live, chosen, 0.0).astype(BF16)
        padded[PAD:PAD + CHUNKS, BOX // 2:BOX // 2 + BOX, :] = jnp.where(is_mine, theirs, ours)

        back = -(BOX * offset[1] + offset[2])
        matrix = shift_matrix(back & (LANES - 1), offset[2])
        window = padded[pl.ds(PAD + (back >> 7), CHUNKS + 1), pl.ds(BOX // 2 - offset[0], BOX), :].astype(BF16)
        moved = jnp.dot(beside(window), matrix, preferred_element_type=F32)
        partner[...] = moved.astype(BF16).reshape(CHUNKS, BOX, LANES)
        density = moved * first[...].reshape(ROWS, LANES).astype(F32)
        along = lanes_dot(density, right_ref[...])
        for chunk in range(0, CHUNKS, 2):
            start = chunk * BOX
            wide = jnp.concatenate([along[start:start + BOX], along[start + BOX:start + 2 * BOX]], axis=1)
            wide = rows_dot(left, wide)
            for part in range(2):
                upper = wide[:BOX // 2, part * LANES:(part + 1) * LANES]
                lower = wide[BOX // 2:, part * LANES:(part + 1) * LANES]
                place = 2 * (chunk + part)
                field[pl.ds(place, BOX // 2, stride=BOX), :] = jnp.where(low, upper, pltpu.roll(lower, BOX, 1))
                field[pl.ds(place + 1, BOX // 2, stride=BOX), :] = jnp.where(low, pltpu.roll(upper, BOX, 1), lower)

        for pos in range(0, ROWS, 2 * BOX):
            wide = jnp.concatenate([field[pos:pos + BOX, :], field[pos + BOX:pos + 2 * BOX, :]], axis=1)
            factor = jnp.concatenate([weight_ref[pos:pos + BOX, :], weight_ref[pos + BOX:pos + 2 * BOX, :]], axis=1)
            wide = rows_dot(left, rows_dot(left, wide) * factor)
            field[pos:pos + BOX, :] = wide[:, :LANES]
            field[pos + BOX:pos + 2 * BOX, :] = wide[:, LANES:]

        pieces = []
        for chunk in range(0, CHUNKS, 2):
            parts = []
            for part in range(2):
                place = 2 * (chunk + part)
                even = field[pl.ds(place, BOX // 2, stride=BOX), :]
                odd = field[pl.ds(place + 1, BOX // 2, stride=BOX), :]
                upper = jnp.where(low, even, pltpu.roll(odd, BOX, 1))
                lower = jnp.where(low, pltpu.roll(even, BOX, 1), odd)
                parts.append(jnp.concatenate([upper, lower], axis=0))
            wide = rows_dot(left, jnp.concatenate(parts, axis=1))
            pieces += [wide[:, :LANES], wide[:, LANES:]]
        potential = lanes_dot(jnp.concatenate(pieces, axis=0), right_ref[...])
        potential = -potential.reshape(CHUNKS, BOX, LANES)
        first_term[...] = potential * partner[...].astype(F32)
        shifted[PAD:PAD + CHUNKS, BOX // 2:BOX // 2 + BOX, :] = potential * first[...].astype(F32)

        ahead = BOX * offset[1] + offset[2]
        matrix = shift_matrix(ahead & (LANES - 1), -offset[2])
        window = shifted[pl.ds(PAD + (ahead >> 7), CHUNKS + 1), pl.ds(BOX // 2 + offset[0], BOX), :]
        high, rest = split(window)
        second_term = jnp.dot(beside(high), matrix, preferred_element_type=F32)
        second_term += jnp.dot(beside(rest), matrix, preferred_element_type=F32)
        second_term = second_term.reshape(CHUNKS, BOX, LANES)
        one = first_term[...]
        total[...] += jnp.where(is_mine, one, second_term)
        sent = jnp.where(is_mine, second_term, one)
        largest = jnp.max(jnp.abs(sent), axis=1, keepdims=True)
        safe = largest > 1e-33
        factor = jnp.where(safe, 32767.0 / jnp.where(safe, largest, 1.0), 0.0)
        coded[edge] = jnp.round(sent * factor).astype(jnp.int32).astype(jnp.int16)
        scales[edge] = (largest * (1.0 / 32767.0)).reshape(CHUNKS, LANES)
        scale_copy(edge, target).start()
        term_copy(edge, target).start()
        return carry

    lax.fori_loop(0, EDGES, pair, 0)

    for edge in range(EDGES):
        scale_copy(edge, users[edge]).wait_recv()
        term_copy(edge, users[edge]).wait_recv()
    for chunk in range(CHUNKS):
        value = total[chunk]
        for edge in range(EDGES):
            value += got[edge, chunk].astype(F32) * got_scales[edge, chunk:chunk + 1, :]
        out_ref[:, chunk * LANES:(chunk + 1) * LANES] = value
    for edge in range(EDGES):
        tab_copy(edge, users[edge]).wait_send()
        box_copy(edge, users[edge]).wait_send()
        scale_copy(edge, targets[edge]).wait_send()
        term_copy(edge, targets[edge]).wait_send()


def body(orbitals, pair_table):
    left, right, weight = tables()
    table = jnp.pad(pair_table.reshape(EDGES, 5), ((0, 4), (0, LANES - 5)), constant_values=-1)
    vmem = pl.BlockSpec(memory_space=pltpu.VMEM)
    cube = (CHUNKS, BOX, LANES)
    wide = (CHUNKS + 2 * PAD, 2 * BOX, LANES)
    dma = pltpu.SemaphoreType.DMA((EDGES,))
    result = pl.pallas_call(
        kernel,
        out_shape=jax.ShapeDtypeStruct((BOX, BOX * BOX), F32),
        in_specs=[vmem] * 5,
        out_specs=vmem,
        scratch_shapes=[
            pltpu.VMEM(cube, BF16),
            pltpu.VMEM((EDGES,) + cube, BF16),
            pltpu.VMEM((EDGES, 8, LANES), jnp.int32),
            pltpu.SMEM((8, LANES), jnp.int32),
            pltpu.SMEM((8, LANES), jnp.int32),
            pltpu.VMEM(wide, F32),
            pltpu.VMEM(wide, F32),
            pltpu.VMEM(cube, BF16),
            pltpu.VMEM(cube, BF16),
            pltpu.VMEM(cube, F32),
            pltpu.VMEM((ROWS, LANES), F32),
            pltpu.VMEM(cube, F32),
            pltpu.VMEM((EDGES,) + cube, jnp.int16),
            pltpu.VMEM((EDGES, CHUNKS, LANES), F32),
            pltpu.VMEM((EDGES,) + cube, jnp.int16),
            pltpu.VMEM((EDGES, CHUNKS, LANES), F32),
            dma, dma, dma, dma, dma, dma, dma, dma,
            pltpu.SemaphoreType.DMA,
        ],
        compiler_params=pltpu.CompilerParams(
            collective_id=0, has_side_effects=True, vmem_limit_bytes=56 * 1024 * 1024),
    )(orbitals.reshape(BOX, BOX * BOX), table, jnp.asarray(left), jnp.asarray(right), jnp.asarray(weight))
    return result.reshape(orbitals.shape)


def solution(mesh):
    in_specs = (P("gx", "gy", None, None, None), P("gx", "gy", None, None))
    out_specs = P("gx", "gy", None, None, None)
    return jax.shard_map(body, mesh=mesh, in_specs=in_specs, out_specs=out_specs, check_vma=False)
```

```python
import math

import jax
import jax.numpy as jnp
import numpy as np
from jax import lax
from jax.experimental import pallas as pl
from jax.experimental.pallas import tpu as pltpu
from jax.sharding import PartitionSpec as P

MESH = pl.DeviceIdType.MESH
F32 = jnp.float32
BF16 = jnp.bfloat16
BOX = 64
LANES = 128
CHUNKS = BOX * BOX // LANES
PAD = 17
ROWS = CHUNKS * BOX
EDGES = 4


def tables():
    cells = np.arange(BOX, dtype=np.float64) + 1
    sine = np.sin(math.pi * cells[:, None] * cells[None, :] / (BOX + 1))
    high = sine.astype(BF16)
    low = (sine - high.astype(np.float64)).astype(BF16)
    none = np.zeros_like(high)
    both = lambda part: np.block([[part, none], [none, part]])
    left = np.concatenate([high, high, low], axis=1)
    right = np.block([[both(high), both(low)], [both(high), both(none)]])
    eigen = 2 - 2 * np.cos(math.pi * cells / (BOX + 1))
    half = np.arange(BOX // 2)[:, None, None]
    middle = np.arange(BOX)[None, :, None]
    lane = np.arange(LANES)[None, None, :]
    total = eigen[lane // BOX * (BOX // 2) + half] + eigen[middle] + eigen[lane % BOX]
    weight = (2 / (BOX + 1)) ** 3 / total
    return left, right, weight.reshape(ROWS, LANES).astype(np.float32)


def split(values):
    high = values.astype(BF16)
    return high, (values - high.astype(F32)).astype(BF16)


def shift_matrix(amount, offset):
    row = lax.broadcasted_iota(jnp.int32, (2 * LANES, LANES), 0)
    col = lax.broadcasted_iota(jnp.int32, (2 * LANES, LANES), 1)
    cell = (col & (BOX - 1)) - offset
    inside = (row == col + amount) & (cell >= 0) & (cell < BOX)
    return jnp.where(inside, 1.0, 0.0).astype(BF16)


def rows_dot(left, values):
    high, low = split(values)
    return jnp.dot(left, jnp.concatenate([high, low, high], axis=0), preferred_element_type=F32)


def lanes_dot(values, right):
    high, low = split(values)
    both = jnp.dot(jnp.concatenate([high, low], axis=1), right, preferred_element_type=F32)
    return both[:, :LANES] + both[:, LANES:]


def beside(chunks):
    before = chunks[:-1].reshape(ROWS, LANES)
    return jnp.concatenate([before, chunks[1:].reshape(ROWS, LANES)], axis=1)


def kernel(
    orb_ref, tab_ref, left_ref, right_ref, weight_ref, out_ref,
    own, near, near_tab, tab_here, tab_near,
    padded, shifted, partner, first, first_term, field, total,
    coded, scales, got, got_scales,
    box_send, box_recv, tab_send, tab_recv, term_send, term_recv, scale_send, scale_recv, local_sem,
):
    span_x, span_y = lax.axis_size("gx"), lax.axis_size("gy")
    here_x, here_y = lax.axis_index("gx"), lax.axis_index("gy")
    core = lax.rem(here_y, 2)

    def at(step_x, step_y):
        return (lax.rem(here_x + step_x + span_x, span_x), lax.rem(here_y + step_y + span_y, span_y))

    def by_core(on_first, on_second):
        return at(*(jnp.where(core == 0, one, two) for one, two in zip(on_first, on_second)))

    targets = [by_core((1, 0), (0, -1)), by_core((0, -1), (-1, 0)), by_core((1, -1), (-1, -1)), by_core((-1, -1), (1, -1))]
    users = [at(0, 1), by_core((-1, 0), (1, 0)), by_core((1, 1), (-1, 1)), by_core((-1, 1), (1, 1))]
    box_slots = [core, core, 2, 3]

    def pick(options, edge):
        chosen = options[0]
        for number in range(1, EDGES):
            chosen = tuple(jnp.where(edge == number, new, old) for new, old in zip(options[number], chosen))
        return chosen

    barrier = pltpu.get_barrier_semaphore()
    for step_x, step_y in ((1, 0), (-1, 0), (0, -1), (1, -1), (-1, -1)):
        pl.semaphore_signal(barrier, inc=1, device_id=at(step_x, step_y), device_id_type=MESH)

    @pl.when(here_y < span_y - 1)
    def _():
        for step_x in (0, 1, -1):
            pl.semaphore_signal(barrier, inc=1, device_id=at(step_x, 1), device_id_type=MESH)

    for chunk in range(CHUNKS):
        own[chunk] = orb_ref[:, chunk * LANES:(chunk + 1) * LANES]
    pl.semaphore_wait(barrier, jnp.where(here_y == 0, 5, 8))

    def tab_copy(edge, slot, device):
        return pltpu.make_async_remote_copy(
            src_ref=tab_ref, dst_ref=near_tab.at[slot], send_sem=tab_send.at[edge],
            recv_sem=tab_recv.at[slot], device_id=device, device_id_type=MESH)

    def box_copy(edge, slot, device):
        return pltpu.make_async_remote_copy(
            src_ref=own, dst_ref=near.at[slot], send_sem=box_send.at[edge],
            recv_sem=box_recv.at[slot], device_id=device, device_id_type=MESH)

    def term_copy(edge, slot, device):
        return pltpu.make_async_remote_copy(
            src_ref=coded.at[edge], dst_ref=got.at[slot], send_sem=term_send.at[edge],
            recv_sem=term_recv.at[slot], device_id=device, device_id_type=MESH)

    def scale_copy(edge, slot, device):
        return pltpu.make_async_remote_copy(
            src_ref=scales.at[edge], dst_ref=got_scales.at[slot], send_sem=scale_send.at[edge],
            recv_sem=scale_recv.at[slot], device_id=device, device_id_type=MESH)

    for edge in range(EDGES):
        tab_copy(edge, box_slots[edge], users[edge]).start()
    for edge in range(2):
        box_copy(edge, box_slots[edge], users[edge]).start()

    local = pltpu.make_async_copy(tab_ref, tab_here, local_sem)
    local.start()
    padded[...] = jnp.zeros_like(padded)
    shifted[...] = jnp.zeros_like(shifted)
    total[...] = jnp.zeros_like(total)
    local.wait()

    left = left_ref[...]
    low = lax.broadcasted_iota(jnp.int32, (BOX // 2, LANES), 1) < BOX
    me = here_x * span_y + here_y

    def pair(edge, carry):
        target = pick(targets, edge)
        other = target[0] * span_y + target[1]
        tab_copy(edge, edge, target).wait_recv()
        copy = pltpu.make_async_copy(near_tab.at[edge], tab_near, local_sem)
        copy.start()
        copy.wait()
        listed = jnp.int32(0)
        wanted = jnp.int32(0)
        offset = [jnp.int32(0)] * 3
        for row in range(EDGES):
            mine = (tab_here[row, 0] == me) & (tab_here[row, 1] == other)
            theirs = (tab_near[row, 0] == other) & (tab_near[row, 1] == me)
            listed = jnp.where(mine, 1, listed)
            wanted = jnp.where(theirs, 1, wanted)
            for dim in range(3):
                value = jnp.where(theirs, tab_near[row, 2 + dim], offset[dim])
                offset[dim] = jnp.where(mine, tab_here[row, 2 + dim], value)
        is_mine = listed == 1
        is_live = (listed + wanted) > 0
        box_copy(edge, edge, target).wait_recv()

        @pl.when(edge == core)
        def _():
            box_copy(2, box_slots[2], users[2]).start()

        @pl.when(edge == core + 1)
        def _():
            box_copy(3, box_slots[3], users[3]).start()

        ours = own[...].astype(F32)
        theirs = near[edge].astype(F32)
        chosen = jnp.where(is_mine, ours, theirs)
        first[...] = jnp.where(is_live, chosen, 0.0).astype(BF16)
        padded[PAD:PAD + CHUNKS, BOX // 2:BOX // 2 + BOX, :] = jnp.where(is_mine, theirs, ours)

        back = -(BOX * offset[1] + offset[2])
        matrix = shift_matrix(back & (LANES - 1), offset[2])
        window = padded[pl.ds(PAD + (back >> 7), CHUNKS + 1), pl.ds(BOX // 2 - offset[0], BOX), :].astype(BF16)
        moved = jnp.dot(beside(window), matrix, preferred_element_type=F32)
        partner[...] = moved.astype(BF16).reshape(CHUNKS, BOX, LANES)
        density = moved * first[...].reshape(ROWS, LANES).astype(F32)
        along = lanes_dot(density, right_ref[...])
        for chunk in range(0, CHUNKS, 2):
            start = chunk * BOX
            wide = jnp.concatenate([along[start:start + BOX], along[start + BOX:start + 2 * BOX]], axis=1)
            wide = rows_dot(left, wide)
            for part in range(2):
                upper = wide[:BOX // 2, part * LANES:(part + 1) * LANES]
                lower = wide[BOX // 2:, part * LANES:(part + 1) * LANES]
                place = 2 * (chunk + part)
                field[pl.ds(place, BOX // 2, stride=BOX), :] = jnp.where(low, upper, pltpu.roll(lower, BOX, 1))
                field[pl.ds(place + 1, BOX // 2, stride=BOX), :] = jnp.where(low, pltpu.roll(upper, BOX, 1), lower)

        for pos in range(0, ROWS, 2 * BOX):
            wide = jnp.concatenate([field[pos:pos + BOX, :], field[pos + BOX:pos + 2 * BOX, :]], axis=1)
            factor = jnp.concatenate([weight_ref[pos:pos + BOX, :], weight_ref[pos + BOX:pos + 2 * BOX, :]], axis=1)
            wide = rows_dot(left, rows_dot(left, wide) * factor)
            field[pos:pos + BOX, :] = wide[:, :LANES]
            field[pos + BOX:pos + 2 * BOX, :] = wide[:, LANES:]

        pieces = []
        for chunk in range(0, CHUNKS, 2):
            parts = []
            for part in range(2):
                place = 2 * (chunk + part)
                even = field[pl.ds(place, BOX // 2, stride=BOX), :]
                odd = field[pl.ds(place + 1, BOX // 2, stride=BOX), :]
                upper = jnp.where(low, even, pltpu.roll(odd, BOX, 1))
                lower = jnp.where(low, pltpu.roll(even, BOX, 1), odd)
                parts.append(jnp.concatenate([upper, lower], axis=0))
            wide = rows_dot(left, jnp.concatenate(parts, axis=1))
            pieces += [wide[:, :LANES], wide[:, LANES:]]
        potential = lanes_dot(jnp.concatenate(pieces, axis=0), right_ref[...])
        potential = -potential.reshape(CHUNKS, BOX, LANES)
        first_term[...] = potential * partner[...].astype(F32)
        shifted[PAD:PAD + CHUNKS, BOX // 2:BOX // 2 + BOX, :] = potential * first[...].astype(F32)

        ahead = BOX * offset[1] + offset[2]
        matrix = shift_matrix(ahead & (LANES - 1), -offset[2])
        window = shifted[pl.ds(PAD + (ahead >> 7), CHUNKS + 1), pl.ds(BOX // 2 + offset[0], BOX), :]
        high, rest = split(window)
        second_term = jnp.dot(beside(high), matrix, preferred_element_type=F32)
        second_term += jnp.dot(beside(rest), matrix, preferred_element_type=F32)
        second_term = second_term.reshape(CHUNKS, BOX, LANES)
        one = first_term[...]
        total[...] += jnp.where(is_mine, one, second_term)
        sent = jnp.where(is_mine, second_term, one)
        largest = jnp.max(jnp.abs(sent), axis=1, keepdims=True)
        safe = largest > 1e-33
        factor = jnp.where(safe, 32767.0 / jnp.where(safe, largest, 1.0), 0.0)
        coded[edge] = jnp.round(sent * factor).astype(jnp.int32).astype(jnp.int16)
        scales[edge] = (largest * (1.0 / 32767.0)).reshape(CHUNKS, LANES)
        term_slot = jnp.where(edge < 2, lax.rem(edge + 1 - core, 2), edge)
        scale_copy(edge, term_slot, target).start()
        term_copy(edge, term_slot, target).start()
        return carry

    lax.fori_loop(0, EDGES, pair, 0)

    for edge in range(EDGES):
        scale_copy(edge, edge, users[edge]).wait_recv()
        term_copy(edge, edge, users[edge]).wait_recv()
    for chunk in range(CHUNKS):
        value = total[chunk]
        for edge in range(EDGES):
            value += got[edge, chunk].astype(F32) * got_scales[edge, chunk:chunk + 1, :]
        out_ref[:, chunk * LANES:(chunk + 1) * LANES] = value
    for edge in range(EDGES):
        tab_copy(edge, edge, users[edge]).wait_send()
        box_copy(edge, edge, users[edge]).wait_send()
        scale_copy(edge, edge, targets[edge]).wait_send()
        term_copy(edge, edge, targets[edge]).wait_send()


def body(orbitals, pair_table):
    left, right, weight = tables()
    table = pair_table.reshape(EDGES, 5)
    vmem = pl.BlockSpec(memory_space=pltpu.VMEM)
    cube = (CHUNKS, BOX, LANES)
    wide = (CHUNKS + 2 * PAD, 2 * BOX, LANES)
    dma = pltpu.SemaphoreType.DMA((EDGES,))
    result = pl.pallas_call(
        kernel,
        out_shape=jax.ShapeDtypeStruct((BOX, BOX * BOX), F32),
        in_specs=[vmem] * 5,
        out_specs=vmem,
        scratch_shapes=[
            pltpu.VMEM(cube, BF16),
            pltpu.VMEM((EDGES,) + cube, BF16),
            pltpu.VMEM((EDGES, EDGES, 5), jnp.int32),
            pltpu.SMEM((EDGES, 5), jnp.int32),
            pltpu.SMEM((EDGES, 5), jnp.int32),
            pltpu.VMEM(wide, F32),
            pltpu.VMEM(wide, F32),
            pltpu.VMEM(cube, BF16),
            pltpu.VMEM(cube, BF16),
            pltpu.VMEM(cube, F32),
            pltpu.VMEM((ROWS, LANES), F32),
            pltpu.VMEM(cube, F32),
            pltpu.VMEM((EDGES,) + cube, jnp.int16),
            pltpu.VMEM((EDGES, CHUNKS, LANES), F32),
            pltpu.VMEM((EDGES,) + cube, jnp.int16),
            pltpu.VMEM((EDGES, CHUNKS, LANES), F32),
            dma, dma, dma, dma, dma, dma, dma, dma,
            pltpu.SemaphoreType.DMA,
        ],
        compiler_params=pltpu.CompilerParams(
            collective_id=0, has_side_effects=True, vmem_limit_bytes=56 * 1024 * 1024),
    )(orbitals.reshape(BOX, BOX * BOX), table, jnp.asarray(left), jnp.asarray(right), jnp.asarray(weight))
    return result.reshape(orbitals.shape)


def solution(mesh):
    in_specs = (P("gx", "gy", None, None, None), P("gx", "gy", None, None))
    out_specs = P("gx", "gy", None, None, None)
    return jax.shard_map(body, mesh=mesh, in_specs=in_specs, out_specs=out_specs, check_vma=False)
```

```python
import math

import jax
import jax.numpy as jnp
import numpy as np
from jax import lax
from jax.experimental import pallas as pl
from jax.experimental.pallas import tpu as pltpu
from jax.sharding import PartitionSpec as P

MESH = pl.DeviceIdType.MESH
F32 = jnp.float32
BF16 = jnp.bfloat16
BOX = 64
HALF = BOX // 2
LANES = 128
CHUNKS = BOX * BOX // LANES
PAD = 17
ROWS = 4
NEAR = 8
GROUP = 16


def tables():
    cells = np.arange(BOX, dtype=np.float64) + 1
    sine = np.sin(math.pi * cells[:, None] * cells[None, :] / (BOX + 1))
    high = sine.astype(BF16)
    low = (sine - high.astype(np.float64)).astype(BF16)
    none = np.zeros_like(high)
    both = lambda part: np.block([[part, none], [none, part]])
    left = np.concatenate([high, high, low], axis=1)
    right = np.block([[both(high), both(low)], [both(high), both(none)]])
    eigen = 2 - 2 * np.cos(math.pi * cells / (BOX + 1))
    row = np.arange(HALF)[:, None]
    lane = np.arange(LANES)[None, :]
    middle = 2 + eigen[lane // BOX * HALF + row] + eigen[lane % BOX]
    ratios = [1 / middle]
    for _ in range(HALF - 1):
        ratios.append(1 / (middle - ratios[-1]))
    ratios.append(1 / (1 - ratios[-1] ** 2))
    return left, right, np.stack(ratios).astype(np.float32)


def split(values):
    high = values.astype(BF16)
    return high, (values - high.astype(F32)).astype(BF16)


def rows_dot(left, values):
    high, low = split(values)
    return jnp.dot(left, jnp.concatenate([high, low, high], axis=0), preferred_element_type=F32)


def lanes_dot(values, right):
    high, low = split(values)
    both = jnp.dot(jnp.concatenate([high, low], axis=1), right, preferred_element_type=F32)
    return both[:, :LANES] + both[:, LANES:]


def shift_masks(amount, offset):
    lane = lax.broadcasted_iota(jnp.int32, (BOX, LANES), 1)
    cell = (lane & (BOX - 1)) - offset
    inside = (cell >= 0) & (cell < BOX)
    return (lane < LANES - amount) & inside, (lane >= LANES - amount) & inside


def shifted(source, slot, chunks, row, flat, offset):
    start, amount = PAD + (flat >> 7), flat & (LANES - 1)
    here, after = shift_masks(amount, offset)
    turned = {}

    def turn(chunk):
        if chunk not in turned:
            values = source[slot, start + chunk, pl.ds(row, BOX), :]
            turned[chunk] = pltpu.roll(values, LANES - amount, 1)
        return turned[chunk]

    return {chunk: jnp.where(here, turn(chunk), jnp.where(after, turn(chunk + 1), 0.0)) for chunk in chunks}


def kernel(
    orb_ref, tab_ref, left_ref, right_ref, ratio_ref, out_ref,
    own, near, tab_here, tab_near, padded, partner, field,
    box_send, box_recv, tab_send, tab_recv, ready, local_sem,
):
    span_x, span_y = lax.axis_size("gx"), lax.axis_size("gy")
    here_x, here_y = lax.axis_index("gx"), lax.axis_index("gy")
    core = lax.rem(here_y, 2)
    sign = 1 - 2 * core

    def at(step_x, step_y):
        return (lax.rem(here_x + step_x + span_x, span_x), lax.rem(here_y + step_y + span_y, span_y))

    twin, beyond, ahead, behind = at(0, sign), at(0, -sign), at(1, 0), at(-1, 0)
    owners = [twin, beyond, ahead, behind, at(1, sign), at(-1, sign), at(1, -sign), at(-1, -sign)]
    dests = [twin, beyond, behind, ahead, twin, twin, beyond, beyond]

    def by_step(step, order):
        slot = order[0]
        for number in range(1, NEAR):
            slot = jnp.where(step == number, order[number], slot)
        return slot

    def pick(slot):
        chosen = owners[0]
        for number in range(1, NEAR):
            chosen = tuple(jnp.where(slot == number, new, old) for new, old in zip(owners[number], chosen))
        return chosen

    asks = jnp.where(core == 0, here_y == 0, here_y < span_y - 1)
    barrier = pltpu.get_barrier_semaphore()
    for device in (twin, ahead, behind):
        pl.semaphore_signal(barrier, inc=1, device_id=device, device_id_type=MESH)

    @pl.when(asks)
    def _():
        pl.semaphore_signal(barrier, inc=1, device_id=beyond, device_id_type=MESH)

    for chunk in range(CHUNKS):
        own[chunk] = orb_ref[:, chunk * LANES:(chunk + 1) * LANES]
    pl.semaphore_wait(barrier, jnp.where(asks, 3, 4))

    def box_copy(slot, source):
        return pltpu.make_async_remote_copy(
            src_ref=source, dst_ref=near.at[slot], send_sem=box_send.at[slot],
            recv_sem=box_recv.at[slot], device_id=dests[slot] if isinstance(slot, int) else twin, device_id_type=MESH)

    def tab_copy(slot, source):
        return pltpu.make_async_remote_copy(
            src_ref=source, dst_ref=tab_near.at[slot], send_sem=tab_send.at[slot],
            recv_sem=tab_recv.at[slot], device_id=dests[slot] if isinstance(slot, int) else twin, device_id_type=MESH)

    def send_own(slot):
        tab_copy(slot, tab_here).start()
        box_copy(slot, own).start()

    def hand_on(slot, source):
        tab_copy(slot, tab_near.at[source]).start()
        box_copy(slot, near.at[source]).start()

    local = pltpu.make_async_copy(tab_ref, tab_here, local_sem)
    local.start()
    local.wait()

    @pl.when(jnp.logical_not(asks))
    def _():
        pl.semaphore_signal(ready, inc=1, device_id=beyond, device_id_type=MESH)

    @pl.when(core == 0)
    def _():
        send_own(3)

    @pl.when(core == 1)
    def _():
        send_own(2)

    send_own(0)

    @pl.when(jnp.logical_not(asks))
    def _():
        send_own(1)

    padded[...] = jnp.zeros_like(padded)
    out_ref[...] = jnp.zeros_like(out_ref)
    padded[0, PAD:PAD + CHUNKS, HALF:HALF + BOX, :] = own[...].astype(F32)

    @pl.when(asks & (core == 1))
    def _():
        pl.semaphore_wait(ready, 1)
        send_own(1)

    left, right = left_ref[...], right_ref[...]
    low = lax.broadcasted_iota(jnp.int32, (HALF, LANES), 1) < BOX
    me = here_x * span_y + here_y

    def pair(step, carry):
        on_first = jnp.where(here_y == 0, by_step(step, (0, 3, 4, 2, 5, 1, 6, 7)), by_step(step, (0, 3, 1, 2, 4, 5, 6, 7)))
        slot = jnp.where(core == 0, on_first, by_step(step, (0, 2, 5, 3, 1, 4, 7, 6)))
        owner = pick(slot)
        other = owner[0] * span_y + owner[1]

        @pl.when((step == 1) & (core == 0))
        def _():
            box_copy(3, own).wait_send()
            send_own(2)

        @pl.when((step == 1) & (core == 1))
        def _():
            box_copy(2, own).wait_send()
            send_own(3)

        @pl.when((step == 1) & (here_y == 0))
        def _():
            pl.semaphore_wait(ready, 1)
            send_own(1)

        tab_copy(slot, tab_here).wait_recv()
        box_copy(slot, own).wait_recv()

        @pl.when(slot == 2)
        def _():
            hand_on(6, 2)
            hand_on(4, 2)

        @pl.when(slot == 3)
        def _():
            hand_on(7, 3)
            hand_on(5, 3)

        listed = jnp.int32(0)
        wanted = jnp.int32(0)
        offset = [jnp.int32(0)] * 3
        for row in range(ROWS):
            mine = (tab_here[row, 0] == me) & (tab_here[row, 1] == other)
            theirs = (tab_near[slot, row, 0] == other) & (tab_near[slot, row, 1] == me)
            listed = jnp.where(mine, 1, listed)
            wanted = jnp.where(theirs, 1, wanted)
            for dim in range(3):
                value = jnp.where(theirs, tab_near[slot, row, 2 + dim], offset[dim])
                offset[dim] = jnp.where(mine, tab_here[row, 2 + dim], value)
        is_mine = listed == 1
        scale = jnp.where(listed + wanted > 0, -((2 / (BOX + 1)) ** 2), 0.0)
        second = listed
        first = 1 - listed
        padded[1, PAD:PAD + CHUNKS, HALF:HALF + BOX, :] = near[slot].astype(F32)

        flat = -(BOX * offset[1] + offset[2])
        order = [chunk for number in range(CHUNKS // 2) for chunk in (number, CHUNKS - 1 - number)]
        front = back = None
        for place in range(0, CHUNKS, GROUP):
            chunks = order[place:place + GROUP]
            moved = shifted(padded, second, sorted(chunks), HALF - offset[0], flat, offset[2])
            products = []
            for chunk in chunks:
                fixed = padded[first, PAD + chunk, HALF:HALF + BOX, :]
                products.append(moved[chunk] * fixed)
                partner[chunk] = jnp.where(is_mine, moved[chunk], fixed).astype(BF16)
            along = lanes_dot(jnp.concatenate(products, axis=0), right)
            for number in range(0, GROUP, 2):
                begin = number * BOX
                wide = jnp.concatenate([along[begin:begin + BOX], along[begin + BOX:begin + 2 * BOX]], axis=1)
                wide = rows_dot(left, wide)
                layers = []
                for part in range(2):
                    upper = wide[:HALF, part * LANES:(part + 1) * LANES]
                    lower = wide[HALF:, part * LANES:(part + 1) * LANES]
                    layers.append(jnp.where(low, upper, pltpu.roll(lower, BOX, 1)))
                    layers.append(jnp.where(low, pltpu.roll(upper, BOX, 1), lower))
                for layer, one, two in ((0, layers[0], layers[3]), (1, layers[1], layers[2])):
                    layer += 2 * chunks[number]
                    if layer > 0:
                        one, two = one + front, two + back
                    front, back = one * ratio_ref[layer], two * ratio_ref[layer]
                    field[layer] = front
                    field[BOX - 1 - layer] = back

        last, closing = ratio_ref[HALF - 1], ratio_ref[HALF]
        solved = {HALF - 1: (front + last * back) * closing, HALF: (back + last * front) * closing}
        order = [chunk for number in reversed(range(CHUNKS // 2)) for chunk in (number, CHUNKS - 1 - number)]
        for place in range(0, CHUNKS, GROUP):
            chunks = order[place:place + GROUP]
            pieces = []
            for number in range(0, GROUP, 2):
                for layer in (2 * chunks[number] + 1, 2 * chunks[number]):
                    if layer < HALF - 1:
                        mirror = BOX - 1 - layer
                        solved[layer] = field[layer] + ratio_ref[layer] * solved[layer + 1]
                        solved[mirror] = field[mirror] + ratio_ref[layer] * solved[mirror - 1]
                parts = []
                for chunk in chunks[number:number + 2]:
                    even, odd = solved[2 * chunk], solved[2 * chunk + 1]
                    upper = jnp.where(low, even, pltpu.roll(odd, BOX, 1))
                    lower = jnp.where(low, pltpu.roll(even, BOX, 1), odd)
                    parts.append(jnp.concatenate([upper, lower], axis=0))
                wide = rows_dot(left, jnp.concatenate(parts, axis=1))
                pieces += [wide[:, :LANES], wide[:, LANES:]]
            potential = lanes_dot(jnp.concatenate(pieces, axis=0), right)
            for number, chunk in enumerate(chunks):
                values = potential[number * BOX:(number + 1) * BOX] * scale
                padded[2, PAD + chunk, HALF:HALF + BOX, :] = values * partner[chunk].astype(F32)

        offset = [jnp.where(is_mine, 0, value) for value in offset]
        flat = BOX * offset[1] + offset[2]
        for place in range(0, CHUNKS, GROUP):
            moved = shifted(padded, 2, range(place, place + GROUP), HALF + offset[0], flat, -offset[2])
            for chunk in range(place, place + GROUP):
                out_ref[:, chunk * LANES:(chunk + 1) * LANES] += moved[chunk]
        return carry

    lax.fori_loop(0, NEAR, pair, 0)

    for slot in range(NEAR):
        source = own if slot < 4 else near.at[2 + slot % 2]
        tab_copy(slot, tab_here).wait_send()
        if slot not in (2, 3):
            box_copy(slot, source).wait_send()

    @pl.when(core == 0)
    def _():
        box_copy(2, own).wait_send()

    @pl.when(core == 1)
    def _():
        box_copy(3, own).wait_send()


def body(orbitals, pair_table):
    left, right, ratios = tables()
    vmem = pl.BlockSpec(memory_space=pltpu.VMEM)
    cube = (CHUNKS, BOX, LANES)
    dma = pltpu.SemaphoreType.DMA((NEAR,))
    result = pl.pallas_call(
        kernel,
        out_shape=jax.ShapeDtypeStruct((BOX, BOX * BOX), F32),
        in_specs=[vmem] * 5,
        out_specs=vmem,
        scratch_shapes=[
            pltpu.VMEM(cube, BF16),
            pltpu.VMEM((NEAR,) + cube, BF16),
            pltpu.SMEM((ROWS, 5), jnp.int32),
            pltpu.SMEM((NEAR, ROWS, 5), jnp.int32),
            pltpu.VMEM((3, CHUNKS + 2 * PAD, 2 * BOX, LANES), F32),
            pltpu.VMEM(cube, BF16),
            pltpu.VMEM((BOX, HALF, LANES), F32),
            dma, dma, dma, dma,
            pltpu.SemaphoreType.REGULAR,
            pltpu.SemaphoreType.DMA,
        ],
        compiler_params=pltpu.CompilerParams(
            collective_id=0, has_side_effects=True, vmem_limit_bytes=56 * 1024 * 1024),
    )(orbitals.reshape(BOX, BOX * BOX), pair_table.reshape(ROWS, 5), jnp.asarray(left), jnp.asarray(right), jnp.asarray(ratios))
    return result.reshape(orbitals.shape)


def solution(mesh):
    in_specs = (P("gx", "gy", None, None, None), P("gx", "gy", None, None))
    out_specs = P("gx", "gy", None, None, None)
    return jax.shard_map(body, mesh=mesh, in_specs=in_specs, out_specs=out_specs, check_vma=False)
```

```python
import math

import jax
import jax.numpy as jnp
import numpy as np
from jax import lax
from jax.experimental import pallas as pl
from jax.experimental.pallas import tpu as pltpu
from jax.sharding import PartitionSpec as P

MESH = pl.DeviceIdType.MESH
F32 = jnp.float32
BF16 = jnp.bfloat16
BOX = 64
HALF = BOX // 2
LANES = 128
CHUNKS = BOX * BOX // LANES
PAD = 17
ROWS = 4
NEAR = 8
GROUP = 16


def tables():
    cells = np.arange(BOX, dtype=np.float64) + 1
    sine = np.sin(math.pi * cells[:, None] * cells[None, :] / (BOX + 1))
    high = sine.astype(BF16)
    low = (sine - high.astype(np.float64)).astype(BF16)
    none = np.zeros_like(high)
    both = lambda part: np.block([[part, none], [none, part]])
    left = np.concatenate([high, high, low], axis=1)
    right = np.block([[both(high), both(low)], [both(high), both(none)]])
    eigen = 2 - 2 * np.cos(math.pi * cells / (BOX + 1))
    row = np.arange(HALF)[:, None]
    lane = np.arange(LANES)[None, :]
    middle = 2 + eigen[lane // BOX * HALF + row] + eigen[lane % BOX]
    ratios = [1 / middle]
    for _ in range(HALF - 1):
        ratios.append(1 / (middle - ratios[-1]))
    ratios.append(1 / (1 - ratios[-1] ** 2))
    return left, right, np.stack(ratios).astype(np.float32)


def split(values):
    high = values.astype(BF16)
    return high, (values - high.astype(F32)).astype(BF16)


def rows_dot(left, values):
    high, low = split(values)
    return jnp.dot(left, jnp.concatenate([high, low, high], axis=0), preferred_element_type=F32)


def lanes_dot(values, right):
    high, low = split(values)
    both = jnp.dot(jnp.concatenate([high, low], axis=1), right, preferred_element_type=F32)
    return both[:, :LANES] + both[:, LANES:]


def shift_masks(amount, offset):
    lane = lax.broadcasted_iota(jnp.int32, (BOX, LANES), 1)
    cell = (lane & (BOX - 1)) - offset
    inside = (cell >= 0) & (cell < BOX)
    return (lane < LANES - amount) & inside, (lane >= LANES - amount) & inside


def shifted(source, slot, chunks, row, flat, offset):
    start, amount = PAD + (flat >> 7), flat & (LANES - 1)
    here, after = shift_masks(amount, offset)
    turned = {}

    def turn(chunk):
        if chunk not in turned:
            values = source[slot, start + chunk, pl.ds(row, BOX), :]
            turned[chunk] = pltpu.roll(values, LANES - amount, 1)
        return turned[chunk]

    return {chunk: jnp.where(here, turn(chunk), jnp.where(after, turn(chunk + 1), 0.0)) for chunk in chunks}


def kernel(
    orb_hbm, tab_hbm, left_hbm, right_hbm, ratio_hbm, out_ref,
    orb_ref, left_ref, right_ref, ratio_ref,
    own, near, tab_here, tab_near, padded, partner, field,
    box_send, box_recv, tab_send, tab_recv, ready, local_sem,
):
    span_x, span_y = lax.axis_size("gx"), lax.axis_size("gy")
    here_x, here_y = lax.axis_index("gx"), lax.axis_index("gy")
    core = lax.rem(here_y, 2)
    sign = 1 - 2 * core

    def at(step_x, step_y):
        return (lax.rem(here_x + step_x + span_x, span_x), lax.rem(here_y + step_y + span_y, span_y))

    twin, beyond, ahead, behind = at(0, sign), at(0, -sign), at(1, 0), at(-1, 0)
    owners = [twin, beyond, ahead, behind, at(1, sign), at(-1, sign), at(1, -sign), at(-1, -sign)]
    dests = [twin, beyond, behind, ahead, twin, twin, beyond, beyond]

    def by_step(step, order):
        slot = order[0]
        for number in range(1, NEAR):
            slot = jnp.where(step == number, order[number], slot)
        return slot

    def pick(slot):
        chosen = owners[0]
        for number in range(1, NEAR):
            chosen = tuple(jnp.where(slot == number, new, old) for new, old in zip(owners[number], chosen))
        return chosen

    barrier = pltpu.get_barrier_semaphore()
    for device in (twin, ahead, behind):
        pl.semaphore_signal(barrier, inc=1, device_id=device, device_id_type=MESH)

    @pl.when(here_y < span_y - 1)
    def _():
        pl.semaphore_signal(barrier, inc=1, device_id=beyond, device_id_type=MESH)

    loads = [
        pltpu.make_async_copy(source, dest, local_sem.at[number])
        for number, (source, dest) in enumerate((
            (orb_hbm, orb_ref), (tab_hbm, tab_here), (left_hbm, left_ref), (right_hbm, right_ref), (ratio_hbm, ratio_ref)))
    ]
    for load in loads:
        load.start()
    loads[0].wait()
    for chunk in range(CHUNKS):
        own[chunk] = orb_ref[:, chunk * LANES:(chunk + 1) * LANES]
    loads[1].wait()
    pl.semaphore_wait(barrier, jnp.where(here_y == 0, 3, 4))

    def box_copy(slot, source):
        return pltpu.make_async_remote_copy(
            src_ref=source, dst_ref=near.at[slot], send_sem=box_send.at[slot],
            recv_sem=box_recv.at[slot], device_id=dests[slot] if isinstance(slot, int) else twin, device_id_type=MESH)

    def tab_copy(slot, source):
        return pltpu.make_async_remote_copy(
            src_ref=source, dst_ref=tab_near.at[slot], send_sem=tab_send.at[slot],
            recv_sem=tab_recv.at[slot], device_id=dests[slot] if isinstance(slot, int) else twin, device_id_type=MESH)

    def send_own(slot):
        tab_copy(slot, tab_here).start()
        box_copy(slot, own).start()

    def hand_on(slot, source):
        tab_copy(slot, tab_near.at[source]).start()
        box_copy(slot, near.at[source]).start()

    @pl.when(here_y == span_y - 1)
    def _():
        pl.semaphore_signal(ready, inc=1, device_id=beyond, device_id_type=MESH)

    @pl.when(here_y > 0)
    def _():
        send_own(1)

    @pl.when(core == 0)
    def _():
        send_own(3)

    @pl.when(core == 1)
    def _():
        send_own(2)

    send_own(0)
    padded[...] = jnp.zeros_like(padded)
    out_ref[...] = jnp.zeros_like(out_ref)
    padded[0, PAD:PAD + CHUNKS, HALF:HALF + BOX, :] = own[...].astype(F32)
    for load in loads[2:]:
        load.wait()

    left, right = left_ref[...], right_ref[...]
    low = lax.broadcasted_iota(jnp.int32, (HALF, LANES), 1) < BOX
    me = here_x * span_y + here_y

    def pair(step, carry):
        on_first = jnp.where(here_y == 0, by_step(step, (0, 3, 4, 2, 5, 1, 6, 7)), by_step(step, (0, 3, 1, 2, 4, 5, 6, 7)))
        slot = jnp.where(core == 0, on_first, by_step(step, (0, 2, 5, 3, 1, 4, 7, 6)))
        owner = pick(slot)
        other = owner[0] * span_y + owner[1]

        @pl.when((step == 1) & (core == 0))
        def _():
            box_copy(3, own).wait_send()
            send_own(2)

        @pl.when((step == 1) & (core == 1))
        def _():
            box_copy(2, own).wait_send()
            send_own(3)

        @pl.when((step == 1) & (here_y == 0))
        def _():
            pl.semaphore_wait(ready, 1)
            send_own(1)

        tab_copy(slot, tab_here).wait_recv()
        box_copy(slot, own).wait_recv()

        @pl.when(slot == 2)
        def _():
            hand_on(6, 2)
            hand_on(4, 2)

        @pl.when(slot == 3)
        def _():
            hand_on(7, 3)
            hand_on(5, 3)

        listed = jnp.int32(0)
        wanted = jnp.int32(0)
        offset = [jnp.int32(0)] * 3
        for row in range(ROWS):
            mine = (tab_here[row, 0] == me) & (tab_here[row, 1] == other)
            theirs = (tab_near[slot, row, 0] == other) & (tab_near[slot, row, 1] == me)
            listed = jnp.where(mine, 1, listed)
            wanted = jnp.where(theirs, 1, wanted)
            for dim in range(3):
                value = jnp.where(theirs, tab_near[slot, row, 2 + dim], offset[dim])
                offset[dim] = jnp.where(mine, tab_here[row, 2 + dim], value)
        is_mine = listed == 1
        scale = jnp.where(listed + wanted > 0, -((2 / (BOX + 1)) ** 2), 0.0)
        second = listed
        first = 1 - listed
        padded[1, PAD:PAD + CHUNKS, HALF:HALF + BOX, :] = near[slot].astype(F32)

        flat = -(BOX * offset[1] + offset[2])
        order = [chunk for number in range(CHUNKS // 2) for chunk in (number, CHUNKS - 1 - number)]
        front = back = None
        for place in range(0, CHUNKS, GROUP):
            chunks = order[place:place + GROUP]
            moved = shifted(padded, second, sorted(chunks), HALF - offset[0], flat, offset[2])
            products = []
            for chunk in chunks:
                fixed = padded[first, PAD + chunk, HALF:HALF + BOX, :]
                products.append(moved[chunk] * fixed)
                partner[chunk] = jnp.where(is_mine, moved[chunk], fixed).astype(BF16)
            along = lanes_dot(jnp.concatenate(products, axis=0), right)
            for number in range(0, GROUP, 2):
                begin = number * BOX
                wide = jnp.concatenate([along[begin:begin + BOX], along[begin + BOX:begin + 2 * BOX]], axis=1)
                wide = rows_dot(left, wide)
                layers = []
                for part in range(2):
                    upper = wide[:HALF, part * LANES:(part + 1) * LANES]
                    lower = wide[HALF:, part * LANES:(part + 1) * LANES]
                    layers.append(jnp.where(low, upper, pltpu.roll(lower, BOX, 1)))
                    layers.append(jnp.where(low, pltpu.roll(upper, BOX, 1), lower))
                for layer, one, two in ((0, layers[0], layers[3]), (1, layers[1], layers[2])):
                    layer += 2 * chunks[number]
                    if layer > 0:
                        one, two = one + front, two + back
                    front, back = one * ratio_ref[layer], two * ratio_ref[layer]
                    field[layer] = front
                    field[BOX - 1 - layer] = back

        last, closing = ratio_ref[HALF - 1], ratio_ref[HALF]
        solved = {HALF - 1: (front + last * back) * closing, HALF: (back + last * front) * closing}
        order = [chunk for number in reversed(range(CHUNKS // 2)) for chunk in (number, CHUNKS - 1 - number)]
        for place in range(0, CHUNKS, GROUP):
            chunks = order[place:place + GROUP]
            pieces = []
            for number in range(0, GROUP, 2):
                for layer in (2 * chunks[number] + 1, 2 * chunks[number]):
                    if layer < HALF - 1:
                        mirror = BOX - 1 - layer
                        solved[layer] = field[layer] + ratio_ref[layer] * solved[layer + 1]
                        solved[mirror] = field[mirror] + ratio_ref[layer] * solved[mirror - 1]
                parts = []
                for chunk in chunks[number:number + 2]:
                    even, odd = solved[2 * chunk], solved[2 * chunk + 1]
                    upper = jnp.where(low, even, pltpu.roll(odd, BOX, 1))
                    lower = jnp.where(low, pltpu.roll(even, BOX, 1), odd)
                    parts.append(jnp.concatenate([upper, lower], axis=0))
                wide = rows_dot(left, jnp.concatenate(parts, axis=1))
                pieces += [wide[:, :LANES], wide[:, LANES:]]
            potential = lanes_dot(jnp.concatenate(pieces, axis=0), right)
            for number, chunk in enumerate(chunks):
                values = potential[number * BOX:(number + 1) * BOX] * scale
                padded[2, PAD + chunk, HALF:HALF + BOX, :] = values * partner[chunk].astype(F32)

        offset = [jnp.where(is_mine, 0, value) for value in offset]
        flat = BOX * offset[1] + offset[2]
        for place in range(0, CHUNKS, GROUP):
            moved = shifted(padded, 2, range(place, place + GROUP), HALF + offset[0], flat, -offset[2])
            for chunk in range(place, place + GROUP):
                out_ref[:, chunk * LANES:(chunk + 1) * LANES] += moved[chunk]
        return carry

    lax.fori_loop(0, NEAR, pair, 0)

    for slot in range(NEAR):
        source = own if slot < 4 else near.at[2 + slot % 2]
        tab_copy(slot, tab_here).wait_send()
        if slot not in (2, 3):
            box_copy(slot, source).wait_send()

    @pl.when(core == 0)
    def _():
        box_copy(2, own).wait_send()

    @pl.when(core == 1)
    def _():
        box_copy(3, own).wait_send()


def body(orbitals, pair_table):
    left, right, ratios = tables()
    operands = [orbitals.reshape(BOX, BOX * BOX), pair_table.reshape(ROWS, 5)]
    operands += [jnp.asarray(table) for table in (left, right, ratios)]
    cube = (CHUNKS, BOX, LANES)
    dma = pltpu.SemaphoreType.DMA((NEAR,))
    result = pl.pallas_call(
        kernel,
        out_shape=pltpu.VMEM((BOX, BOX * BOX), F32),
        in_specs=[pl.BlockSpec(memory_space=pltpu.HBM)] * 5,
        out_specs=pl.BlockSpec(memory_space=pltpu.VMEM),
        scratch_shapes=[
            pltpu.VMEM((BOX, BOX * BOX), BF16),
            pltpu.VMEM(left.shape, BF16),
            pltpu.VMEM(right.shape, BF16),
            pltpu.VMEM(ratios.shape, F32),
            pltpu.VMEM(cube, BF16),
            pltpu.VMEM((NEAR,) + cube, BF16),
            pltpu.SMEM((ROWS, 5), jnp.int32),
            pltpu.SMEM((NEAR, ROWS, 5), jnp.int32),
            pltpu.VMEM((3, CHUNKS + 2 * PAD, 2 * BOX, LANES), F32),
            pltpu.VMEM(cube, BF16),
            pltpu.VMEM((BOX, HALF, LANES), F32),
            dma, dma, dma, dma,
            pltpu.SemaphoreType.REGULAR,
            pltpu.SemaphoreType.DMA((5,)),
        ],
        compiler_params=pltpu.CompilerParams(
            collective_id=0, has_side_effects=True, vmem_limit_bytes=32 * 1024 * 1024),
    )(*(pltpu.with_memory_space_constraint(operand, pltpu.HBM) for operand in operands))
    return result.reshape(orbitals.shape)


def solution(mesh):
    in_specs = (P("gx", "gy", None, None, None), P("gx", "gy", None, None))
    out_specs = P("gx", "gy", None, None, None)
    return jax.shard_map(body, mesh=mesh, in_specs=in_specs, out_specs=out_specs, check_vma=False)
```

```python
import math

import jax
import jax.numpy as jnp
import numpy as np
from jax import lax
from jax.experimental import pallas as pl
from jax.experimental.pallas import tpu as pltpu
from jax.sharding import PartitionSpec as P

MESH = pl.DeviceIdType.MESH
F32 = jnp.float32
BF16 = jnp.bfloat16
BOX = 64
HALF = BOX // 2
LANES = 128
CHUNKS = BOX * BOX // LANES
PAD = 17
ROWS = 4
NEAR = 8
GROUP = 32


def tables():
    cells = np.arange(BOX, dtype=np.float64) + 1
    sine = np.sin(math.pi * cells[:, None] * cells[None, :] / (BOX + 1))
    high = sine.astype(BF16)
    low = (sine - high.astype(np.float64)).astype(BF16)
    none = np.zeros_like(high)
    both = lambda part: np.block([[part, none], [none, part]])
    left = np.concatenate([high, high, low], axis=1)
    right = np.block([[both(high), both(low)], [both(high), both(none)]])
    eigen = 2 - 2 * np.cos(math.pi * cells / (BOX + 1))
    row = np.arange(HALF)[:, None]
    lane = np.arange(LANES)[None, :]
    middle = 2 + eigen[lane // BOX * HALF + row] + eigen[lane % BOX]
    ratios = [1 / middle]
    for _ in range(HALF - 1):
        ratios.append(1 / (middle - ratios[-1]))
    ratios.append(1 / (1 - ratios[-1] ** 2))
    return left, right, np.stack(ratios).astype(np.float32)


def split(values):
    high = values.astype(BF16)
    return high, (values - high.astype(F32)).astype(BF16)


def rows_dot(left, values):
    high, low = split(values)
    return jnp.dot(left, jnp.concatenate([high, low, high], axis=0), preferred_element_type=F32)


def lanes_dot(values, right):
    high, low = split(values)
    both = jnp.dot(jnp.concatenate([high, low], axis=1), right, preferred_element_type=F32)
    return both[:, :LANES] + both[:, LANES:]


def shift_masks(amount, offset):
    lane = lax.broadcasted_iota(jnp.int32, (BOX, LANES), 1)
    cell = (lane & (BOX - 1)) - offset
    inside = (cell >= 0) & (cell < BOX)
    return (lane < LANES - amount) & inside, (lane >= LANES - amount) & inside


def shifted(source, slot, chunks, row, flat, offset):
    start, amount = PAD + (flat >> 7), flat & (LANES - 1)
    here, after = shift_masks(amount, offset)
    turned = {}

    def turn(chunk):
        if chunk not in turned:
            values = source[slot, start + chunk, pl.ds(row, BOX), :]
            turned[chunk] = pltpu.roll(values, LANES - amount, 1)
        return turned[chunk]

    return {chunk: jnp.where(here, turn(chunk), jnp.where(after, turn(chunk + 1), 0.0)) for chunk in chunks}


def kernel(
    orb_hbm, tab_hbm, left_hbm, right_hbm, ratio_hbm, out_ref,
    orb_ref, left_ref, right_ref, ratio_ref,
    own, near, tab_here, tab_near, padded, partner, field,
    box_send, box_recv, tab_send, tab_recv, ready, local_sem,
):
    span_x, span_y = lax.axis_size("gx"), lax.axis_size("gy")
    here_x, here_y = lax.axis_index("gx"), lax.axis_index("gy")
    core = lax.rem(here_y, 2)
    sign = 1 - 2 * core

    def at(step_x, step_y):
        return (lax.rem(here_x + step_x + span_x, span_x), lax.rem(here_y + step_y + span_y, span_y))

    twin, beyond, ahead, behind = at(0, sign), at(0, -sign), at(1, 0), at(-1, 0)
    owners = [twin, beyond, ahead, behind, at(1, sign), at(-1, sign), at(1, -sign), at(-1, -sign)]
    dests = [twin, beyond, behind, ahead, twin, twin, beyond, beyond]

    def by_step(step, order):
        slot = order[0]
        for number in range(1, NEAR):
            slot = jnp.where(step == number, order[number], slot)
        return slot

    def pick(slot):
        chosen = owners[0]
        for number in range(1, NEAR):
            chosen = tuple(jnp.where(slot == number, new, old) for new, old in zip(owners[number], chosen))
        return chosen

    barrier = pltpu.get_barrier_semaphore()
    for device in (ahead, behind):
        pl.semaphore_signal(barrier, inc=1, device_id=device, device_id_type=MESH)
    for signals, device in ((core == 1, twin), (here_y < span_y - 1, beyond)):
        @pl.when(signals)
        def _():
            pl.semaphore_signal(barrier, inc=1, device_id=device, device_id_type=MESH)

    loads = [
        pltpu.make_async_copy(source, dest, local_sem.at[number])
        for number, (source, dest) in enumerate((
            (orb_hbm, orb_ref), (tab_hbm, tab_here), (left_hbm, left_ref), (right_hbm, right_ref), (ratio_hbm, ratio_ref)))
    ]
    for load in loads:
        load.start()
    loads[0].wait()
    for chunk in range(CHUNKS):
        own[chunk] = orb_ref[:, chunk * LANES:(chunk + 1) * LANES]
    loads[1].wait()
    pl.semaphore_wait(barrier, 2 + jnp.where(core == 0, 1, 0) + jnp.where(here_y == 0, 0, 1))
    for answers, device, number in ((core == 0, twin, 0), (here_y == span_y - 1, beyond, 1)):
        @pl.when(answers)
        def _():
            pl.semaphore_signal(ready.at[number], inc=1, device_id=device, device_id_type=MESH)

    def box_copy(slot, source):
        return pltpu.make_async_remote_copy(
            src_ref=source, dst_ref=near.at[slot], send_sem=box_send.at[slot],
            recv_sem=box_recv.at[slot], device_id=dests[slot] if isinstance(slot, int) else twin, device_id_type=MESH)

    def tab_copy(slot, source):
        return pltpu.make_async_remote_copy(
            src_ref=source, dst_ref=tab_near.at[slot], send_sem=tab_send.at[slot],
            recv_sem=tab_recv.at[slot], device_id=dests[slot] if isinstance(slot, int) else twin, device_id_type=MESH)

    def send_own(slot):
        tab_copy(slot, tab_here).start()
        box_copy(slot, own).start()

    def hand_on(slot, source):
        tab_copy(slot, tab_near.at[source]).start()
        box_copy(slot, near.at[source]).start()

    def pass_on(slot, device):
        return [
            pltpu.make_async_remote_copy(
                src_ref=here.at[1], dst_ref=here.at[slot], send_sem=send.at[NEAR + slot - 6],
                recv_sem=recv.at[slot], device_id=device, device_id_type=MESH)
            for here, send, recv in ((tab_near, tab_send, tab_recv), (near, box_send, box_recv))
        ]

    twin_last = (here_x == 0) & (here_y == 1)

    def send_twin():
        pl.semaphore_wait(ready.at[0], 1)
        send_own(0)

    @pl.when(here_y > 0)
    def _():
        send_own(1)

    @pl.when(core == 0)
    def _():
        send_own(3)
        send_own(0)

    @pl.when(core == 1)
    def _():
        send_own(2)

    padded[...] = jnp.zeros_like(padded)
    out_ref[...] = jnp.zeros_like(out_ref)
    padded[0, PAD:PAD + CHUNKS, HALF:HALF + BOX, :] = own[...].astype(F32)

    @pl.when((core == 1) & jnp.logical_not(twin_last))
    def _():
        send_twin()

    for load in loads[2:]:
        load.wait()

    hands_behind = ((core == 1) & (here_y < span_y - 1)) | (here_y == 2)
    passes_behind = ((core == 1) & (here_y != 1)) | (here_y == 0)
    left, right = left_ref[...], right_ref[...]
    low = lax.broadcasted_iota(jnp.int32, (HALF, LANES), 1) < BOX
    me = here_x * span_y + here_y

    def pair(step, carry):
        on_first = jnp.where(here_y == 0, by_step(step, (0, 3, 4, 1, 2, 5, 6, 7)), by_step(step, (0, 3, 1, 4, 2, 6, 5, 7)))
        on_second = jnp.where(twin_last, by_step(step, (2, 1, 0, 5, 3, 7, 4, 6)), by_step(step, (0, 2, 5, 1, 3, 7, 4, 6)))
        slot = jnp.where(core == 0, on_first, on_second)
        owner = pick(slot)
        other = owner[0] * span_y + owner[1]

        @pl.when((step == 1) & (core == 0))
        def _():
            box_copy(3, own).wait_send()
            send_own(2)

        @pl.when((step == 1) & (core == 1))
        def _():
            box_copy(2, own).wait_send()
            send_own(3)

        @pl.when((step == 1) & (here_y == 0))
        def _():
            pl.semaphore_wait(ready.at[1], 1)
            send_own(1)

        tab_copy(slot, tab_here).wait_recv()
        box_copy(slot, own).wait_recv()

        @pl.when((slot == 2) & twin_last)
        def _():
            send_twin()

        @pl.when((slot == 2) & hands_behind)
        def _():
            hand_on(6, 2)

        @pl.when((slot == 3) & (core == 0))
        def _():
            hand_on(7, 3)

        for first_hop, inward in ((2, 4), (3, 5)):
            @pl.when(slot == first_hop)
            def _():
                hand_on(inward, first_hop)

        @pl.when((slot == 1) & (core == 0))
        def _():
            for copy in pass_on(7, ahead):
                copy.start()

        @pl.when((slot == 1) & passes_behind)
        def _():
            for copy in pass_on(6, behind):
                copy.start()

        listed = jnp.int32(0)
        wanted = jnp.int32(0)
        offset = [jnp.int32(0)] * 3
        for row in range(ROWS):
            mine = (tab_here[row, 0] == me) & (tab_here[row, 1] == other)
            theirs = (tab_near[slot, row, 0] == other) & (tab_near[slot, row, 1] == me)
            listed = jnp.where(mine, 1, listed)
            wanted = jnp.where(theirs, 1, wanted)
            for dim in range(3):
                value = jnp.where(theirs, tab_near[slot, row, 2 + dim], offset[dim])
                offset[dim] = jnp.where(mine, tab_here[row, 2 + dim], value)
        is_mine = listed == 1
        scale = jnp.where(listed + wanted > 0, -((2 / (BOX + 1)) ** 2), 0.0)
        second = listed
        first = 1 - listed
        padded[1, PAD:PAD + CHUNKS, HALF:HALF + BOX, :] = near[slot].astype(F32)

        flat = -(BOX * offset[1] + offset[2])
        order = [chunk for number in range(CHUNKS // 2) for chunk in (number, CHUNKS - 1 - number)]
        front = back = None
        for place in range(0, CHUNKS, GROUP):
            chunks = order[place:place + GROUP]
            moved = shifted(padded, second, sorted(chunks), HALF - offset[0], flat, offset[2])
            products = []
            for chunk in chunks:
                fixed = padded[first, PAD + chunk, HALF:HALF + BOX, :]
                products.append(moved[chunk] * fixed)
                partner[chunk] = jnp.where(is_mine, moved[chunk], fixed).astype(BF16)
            along = lanes_dot(jnp.concatenate(products, axis=0), right)
            for number in range(0, GROUP, 2):
                begin = number * BOX
                wide = jnp.concatenate([along[begin:begin + BOX], along[begin + BOX:begin + 2 * BOX]], axis=1)
                wide = rows_dot(left, wide)
                layers = []
                for part in range(2):
                    upper = wide[:HALF, part * LANES:(part + 1) * LANES]
                    lower = wide[HALF:, part * LANES:(part + 1) * LANES]
                    layers.append(jnp.where(low, upper, pltpu.roll(lower, BOX, 1)))
                    layers.append(jnp.where(low, pltpu.roll(upper, BOX, 1), lower))
                for layer, one, two in ((0, layers[0], layers[3]), (1, layers[1], layers[2])):
                    layer += 2 * chunks[number]
                    if layer > 0:
                        one, two = one + front, two + back
                    front, back = one * ratio_ref[layer], two * ratio_ref[layer]
                    field[layer] = front
                    field[BOX - 1 - layer] = back

        last, closing = ratio_ref[HALF - 1], ratio_ref[HALF]
        solved = {HALF - 1: (front + last * back) * closing, HALF: (back + last * front) * closing}
        order = [chunk for number in reversed(range(CHUNKS // 2)) for chunk in (number, CHUNKS - 1 - number)]
        for place in range(0, CHUNKS, GROUP):
            chunks = order[place:place + GROUP]
            pieces = []
            for number in range(0, GROUP, 2):
                for layer in (2 * chunks[number] + 1, 2 * chunks[number]):
                    if layer < HALF - 1:
                        mirror = BOX - 1 - layer
                        solved[layer] = field[layer] + ratio_ref[layer] * solved[layer + 1]
                        solved[mirror] = field[mirror] + ratio_ref[layer] * solved[mirror - 1]
                parts = []
                for chunk in chunks[number:number + 2]:
                    even, odd = solved[2 * chunk], solved[2 * chunk + 1]
                    upper = jnp.where(low, even, pltpu.roll(odd, BOX, 1))
                    lower = jnp.where(low, pltpu.roll(even, BOX, 1), odd)
                    parts.append(jnp.concatenate([upper, lower], axis=0))
                wide = rows_dot(left, jnp.concatenate(parts, axis=1))
                pieces += [wide[:, :LANES], wide[:, LANES:]]
            potential = lanes_dot(jnp.concatenate(pieces, axis=0), right)
            for number, chunk in enumerate(chunks):
                values = potential[number * BOX:(number + 1) * BOX] * scale
                padded[2, PAD + chunk, HALF:HALF + BOX, :] = values * partner[chunk].astype(F32)

        offset = [jnp.where(is_mine, 0, value) for value in offset]
        flat = BOX * offset[1] + offset[2]
        for place in range(0, CHUNKS, GROUP):
            moved = shifted(padded, 2, range(place, place + GROUP), HALF + offset[0], flat, -offset[2])
            for chunk in range(place, place + GROUP):
                out_ref[:, chunk * LANES:(chunk + 1) * LANES] += moved[chunk]
        return carry

    lax.fori_loop(0, NEAR, pair, 0)

    for slot in range(NEAR):
        source = own if slot < 4 else near.at[2 + slot % 2]
        if slot < 6:
            tab_copy(slot, tab_here).wait_send()
        if slot not in (2, 3, 6, 7):
            box_copy(slot, source).wait_send()

    for holds, slot in ((hands_behind, 6), (core == 0, 7)):
        @pl.when(holds)
        def _():
            tab_copy(slot, tab_here).wait_send()
            box_copy(slot, own).wait_send()

    for holds, copies in ((core == 0, pass_on(7, ahead)), (passes_behind, pass_on(6, behind))):
        @pl.when(holds)
        def _():
            for copy in copies:
                copy.wait_send()

    @pl.when(core == 0)
    def _():
        box_copy(2, own).wait_send()

    @pl.when(core == 1)
    def _():
        box_copy(3, own).wait_send()


def body(orbitals, pair_table):
    left, right, ratios = tables()
    operands = [orbitals.reshape(BOX, BOX * BOX), pair_table.reshape(ROWS, 5)]
    operands += [jnp.asarray(table) for table in (left, right, ratios)]
    cube = (CHUNKS, BOX, LANES)
    dma = pltpu.SemaphoreType.DMA((NEAR + 2,))
    result = pl.pallas_call(
        kernel,
        out_shape=pltpu.VMEM((BOX, BOX * BOX), F32),
        in_specs=[pl.BlockSpec(memory_space=pltpu.HBM)] * 5,
        out_specs=pl.BlockSpec(memory_space=pltpu.VMEM),
        scratch_shapes=[
            pltpu.VMEM((BOX, BOX * BOX), BF16),
            pltpu.VMEM(left.shape, BF16),
            pltpu.VMEM(right.shape, BF16),
            pltpu.VMEM(ratios.shape, F32),
            pltpu.VMEM(cube, BF16),
            pltpu.VMEM((NEAR,) + cube, BF16),
            pltpu.SMEM((ROWS, 5), jnp.int32),
            pltpu.SMEM((NEAR, ROWS, 5), jnp.int32),
            pltpu.VMEM((3, CHUNKS + 2 * PAD, 2 * BOX, LANES), F32),
            pltpu.VMEM(cube, BF16),
            pltpu.VMEM((BOX, HALF, LANES), F32),
            dma, dma, dma, dma,
            pltpu.SemaphoreType.REGULAR((2,)),
            pltpu.SemaphoreType.DMA((5,)),
        ],
        compiler_params=pltpu.CompilerParams(
            collective_id=0, has_side_effects=True, vmem_limit_bytes=32 * 1024 * 1024),
    )(*(pltpu.with_memory_space_constraint(operand, pltpu.HBM) for operand in operands))
    return result.reshape(orbitals.shape)


def solution(mesh):
    in_specs = (P("gx", "gy", None, None, None), P("gx", "gy", None, None))
    out_specs = P("gx", "gy", None, None, None)
    return jax.shard_map(body, mesh=mesh, in_specs=in_specs, out_specs=out_specs, check_vma=False)
```

```python
import math

import jax
import jax.numpy as jnp
import numpy as np
from jax import lax
from jax.experimental import pallas as pl
from jax.experimental.pallas import tpu as pltpu
from jax.sharding import PartitionSpec as P

MESH = pl.DeviceIdType.MESH
F32 = jnp.float32
BF16 = jnp.bfloat16
BOX = 64
HALF = BOX // 2
LANES = 128
CHUNKS = BOX * BOX // LANES
PAD = 17
ROWS = 4
NEAR = 8
GROUP = 32


def tables():
    cells = np.arange(BOX, dtype=np.float64) + 1
    sine = np.sin(math.pi * cells[:, None] * cells[None, :] / (BOX + 1))
    high = sine.astype(BF16)
    low = (sine - high.astype(np.float64)).astype(BF16)
    none = np.zeros_like(high)
    both = lambda part: np.block([[part, none], [none, part]])
    left = np.concatenate([high, high, low], axis=1)
    right = np.block([[both(high), both(low)], [both(high), both(none)]])
    eigen = 2 - 2 * np.cos(math.pi * cells / (BOX + 1))
    row = np.arange(HALF)[:, None]
    lane = np.arange(LANES)[None, :]
    middle = 2 + eigen[lane // BOX * HALF + row] + eigen[lane % BOX]
    ratios = [1 / middle]
    for _ in range(HALF - 1):
        ratios.append(1 / (middle - ratios[-1]))
    ratios.append(1 / (1 - ratios[-1] ** 2))
    return left, right, np.stack(ratios).astype(np.float32)


def split(values):
    high = values.astype(BF16)
    return high, (values - high.astype(F32)).astype(BF16)


def rows_dot(left, values):
    high, low = split(values)
    return jnp.dot(left, jnp.concatenate([high, low, high], axis=0), preferred_element_type=F32)


def lanes_dot(values, right):
    high, low = split(values)
    both = jnp.dot(jnp.concatenate([high, low], axis=1), right, preferred_element_type=F32)
    return both[:, :LANES] + both[:, LANES:]


def shift_masks(amount, offset):
    lane = lax.broadcasted_iota(jnp.int32, (BOX, LANES), 1)
    cell = (lane & (BOX - 1)) - offset
    inside = (cell >= 0) & (cell < BOX)
    return (lane < LANES - amount) & inside, (lane >= LANES - amount) & inside


def shifted(source, slot, chunks, row, flat, offset):
    start, amount = PAD + (flat >> 7), flat & (LANES - 1)
    here, after = shift_masks(amount, offset)
    turned = {}

    def turn(chunk):
        if chunk not in turned:
            values = source[slot, start + chunk, pl.ds(row, BOX), :]
            turned[chunk] = pltpu.roll(values, LANES - amount, 1)
        return turned[chunk]

    return {chunk: jnp.where(here, turn(chunk), jnp.where(after, turn(chunk + 1), 0.0)) for chunk in chunks}


def kernel(
    orb_hbm, tab_hbm, left_hbm, right_hbm, ratio_hbm, out_ref,
    orb_ref, left_ref, right_ref, ratio_ref,
    own, near, tab_here, tab_near, padded, partner, field,
    box_send, box_recv, tab_send, tab_recv, ready, local_sem,
):
    span_x, span_y = lax.axis_size("gx"), lax.axis_size("gy")
    here_x, here_y = lax.axis_index("gx"), lax.axis_index("gy")
    core = lax.rem(here_y, 2)
    sign = 1 - 2 * core

    def at(step_x, step_y):
        return (lax.rem(here_x + step_x + span_x, span_x), lax.rem(here_y + step_y + span_y, span_y))

    twin, beyond, ahead, behind = at(0, sign), at(0, -sign), at(1, 0), at(-1, 0)
    owners = [twin, beyond, ahead, behind, at(1, sign), at(-1, sign), at(1, -sign), at(-1, -sign)]
    dests = [twin, beyond, behind, ahead, twin, twin, beyond, beyond]

    def by_step(step, order):
        slot = order[0]
        for number in range(1, NEAR):
            slot = jnp.where(step == number, order[number], slot)
        return slot

    def pick(slot):
        chosen = owners[0]
        for number in range(1, NEAR):
            chosen = tuple(jnp.where(slot == number, new, old) for new, old in zip(owners[number], chosen))
        return chosen

    barrier = pltpu.get_barrier_semaphore()
    for device in (ahead, behind):
        pl.semaphore_signal(barrier, inc=1, device_id=device, device_id_type=MESH)
    for signals, device in ((core == 1, twin), (here_y < span_y - 1, beyond)):
        @pl.when(signals)
        def _():
            pl.semaphore_signal(barrier, inc=1, device_id=device, device_id_type=MESH)

    loads = [
        pltpu.make_async_copy(source, dest, local_sem.at[number])
        for number, (source, dest) in enumerate((
            (orb_hbm, orb_ref), (tab_hbm, tab_here), (left_hbm, left_ref), (right_hbm, right_ref), (ratio_hbm, ratio_ref)))
    ]
    for load in loads:
        load.start()
    loads[0].wait()
    for chunk in range(CHUNKS):
        own[chunk] = orb_ref[:, chunk * LANES:(chunk + 1) * LANES]
    loads[1].wait()
    pl.semaphore_wait(barrier, 2 + jnp.where(core == 0, 1, 0) + jnp.where(here_y == 0, 0, 1))
    for answers, device, number in ((core == 0, twin, 0), (here_y == span_y - 1, beyond, 1)):
        @pl.when(answers)
        def _():
            pl.semaphore_signal(ready.at[number], inc=1, device_id=device, device_id_type=MESH)

    def box_copy(slot, source):
        return pltpu.make_async_remote_copy(
            src_ref=source, dst_ref=near.at[slot], send_sem=box_send.at[slot],
            recv_sem=box_recv.at[slot], device_id=dests[slot] if isinstance(slot, int) else twin, device_id_type=MESH)

    def tab_copy(slot, source):
        return pltpu.make_async_remote_copy(
            src_ref=source, dst_ref=tab_near.at[slot], send_sem=tab_send.at[slot],
            recv_sem=tab_recv.at[slot], device_id=dests[slot] if isinstance(slot, int) else twin, device_id_type=MESH)

    def send_own(slot):
        tab_copy(slot, tab_here).start()
        box_copy(slot, own).start()

    def hand_on(slot, source):
        tab_copy(slot, tab_near.at[source]).start()
        box_copy(slot, near.at[source]).start()

    def pass_on(slot, device):
        return [
            pltpu.make_async_remote_copy(
                src_ref=here.at[1], dst_ref=here.at[slot], send_sem=send.at[NEAR + slot - 6],
                recv_sem=recv.at[slot], device_id=device, device_id_type=MESH)
            for here, send, recv in ((tab_near, tab_send, tab_recv), (near, box_send, box_recv))
        ]

    twin_last = (here_x == 0) & (here_y == 1)

    def send_twin():
        pl.semaphore_wait(ready.at[0], 1)
        send_own(0)

    @pl.when(here_y > 0)
    def _():
        send_own(1)

    @pl.when(core == 0)
    def _():
        send_own(3)
        send_own(0)

    @pl.when(core == 1)
    def _():
        send_own(2)

    padded[...] = jnp.zeros_like(padded)
    out_ref[...] = jnp.zeros_like(out_ref)
    padded[0, PAD:PAD + CHUNKS, HALF:HALF + BOX, :] = own[...].astype(F32)

    @pl.when((core == 1) & jnp.logical_not(twin_last))
    def _():
        send_twin()

    for load in loads[2:]:
        load.wait()

    hands_behind = ((core == 1) & (here_y < span_y - 1)) | (here_y == 2)
    passes_behind = ((core == 1) & (here_y != 1)) | (here_y == 0)
    left, right = left_ref[...], right_ref[...]
    low = lax.broadcasted_iota(jnp.int32, (HALF, LANES), 1) < BOX
    me = here_x * span_y + here_y

    def pair(step, carry):
        on_first = jnp.where(here_y == 0, jnp.where(here_x == span_x - 1, by_step(step, (0, 3, 4, 1, 2, 5, 7, 6)), by_step(step, (0, 3, 4, 1, 2, 5, 6, 7))), by_step(step, (0, 3, 1, 4, 2, 6, 5, 7)))
        on_second = jnp.where(twin_last, by_step(step, (2, 1, 0, 5, 3, 7, 4, 6)), by_step(step, (0, 2, 5, 1, 3, 7, 4, 6)))
        slot = jnp.where(core == 0, on_first, on_second)
        owner = pick(slot)
        other = owner[0] * span_y + owner[1]

        @pl.when((step == 1) & (core == 0))
        def _():
            box_copy(3, own).wait_send()
            send_own(2)

        @pl.when((step == 1) & (core == 1))
        def _():
            box_copy(2, own).wait_send()
            send_own(3)

        @pl.when((step == 1) & (here_y == 0))
        def _():
            pl.semaphore_wait(ready.at[1], 1)
            send_own(1)

        tab_copy(slot, tab_here).wait_recv()
        box_copy(slot, own).wait_recv()

        @pl.when((slot == 2) & twin_last)
        def _():
            send_twin()

        @pl.when((slot == 2) & hands_behind)
        def _():
            hand_on(6, 2)

        @pl.when((slot == 3) & (core == 0))
        def _():
            hand_on(7, 3)

        for first_hop, inward in ((2, 4), (3, 5)):
            @pl.when(slot == first_hop)
            def _():
                hand_on(inward, first_hop)

        @pl.when((slot == 1) & (core == 0))
        def _():
            for copy in pass_on(7, ahead):
                copy.start()

        @pl.when((slot == 1) & passes_behind)
        def _():
            for copy in pass_on(6, behind):
                copy.start()

        listed = jnp.int32(0)
        wanted = jnp.int32(0)
        offset = [jnp.int32(0)] * 3
        for row in range(ROWS):
            mine = (tab_here[row, 0] == me) & (tab_here[row, 1] == other)
            theirs = (tab_near[slot, row, 0] == other) & (tab_near[slot, row, 1] == me)
            listed = jnp.where(mine, 1, listed)
            wanted = jnp.where(theirs, 1, wanted)
            for dim in range(3):
                value = jnp.where(theirs, tab_near[slot, row, 2 + dim], offset[dim])
                offset[dim] = jnp.where(mine, tab_here[row, 2 + dim], value)
        is_mine = listed == 1
        scale = jnp.where(listed + wanted > 0, -((2 / (BOX + 1)) ** 2), 0.0)
        second = listed
        first = 1 - listed
        padded[1, PAD:PAD + CHUNKS, HALF:HALF + BOX, :] = near[slot].astype(F32)

        flat = -(BOX * offset[1] + offset[2])
        order = [chunk for number in range(CHUNKS // 2) for chunk in (number, CHUNKS - 1 - number)]
        front = back = None
        for place in range(0, CHUNKS, GROUP):
            chunks = order[place:place + GROUP]
            moved = shifted(padded, second, sorted(chunks), HALF - offset[0], flat, offset[2])
            products = []
            for chunk in chunks:
                fixed = padded[first, PAD + chunk, HALF:HALF + BOX, :]
                products.append(moved[chunk] * fixed)
                partner[chunk] = jnp.where(is_mine, moved[chunk], fixed).astype(BF16)
            along = lanes_dot(jnp.concatenate(products, axis=0), right)
            for number in range(0, GROUP, 2):
                begin = number * BOX
                wide = jnp.concatenate([along[begin:begin + BOX], along[begin + BOX:begin + 2 * BOX]], axis=1)
                wide = rows_dot(left, wide)
                layers = []
                for part in range(2):
                    upper = wide[:HALF, part * LANES:(part + 1) * LANES]
                    lower = wide[HALF:, part * LANES:(part + 1) * LANES]
                    layers.append(jnp.where(low, upper, pltpu.roll(lower, BOX, 1)))
                    layers.append(jnp.where(low, pltpu.roll(upper, BOX, 1), lower))
                for layer, one, two in ((0, layers[0], layers[3]), (1, layers[1], layers[2])):
                    layer += 2 * chunks[number]
                    if layer > 0:
                        one, two = one + front, two + back
                    front, back = one * ratio_ref[layer], two * ratio_ref[layer]
                    field[layer] = front
                    field[BOX - 1 - layer] = back

        last, closing = ratio_ref[HALF - 1], ratio_ref[HALF]
        solved = {HALF - 1: (front + last * back) * closing, HALF: (back + last * front) * closing}
        order = [chunk for number in reversed(range(CHUNKS // 2)) for chunk in (number, CHUNKS - 1 - number)]
        for place in range(0, CHUNKS, GROUP):
            chunks = order[place:place + GROUP]
            pieces = []
            for number in range(0, GROUP, 2):
                for layer in (2 * chunks[number] + 1, 2 * chunks[number]):
                    if layer < HALF - 1:
                        mirror = BOX - 1 - layer
                        solved[layer] = field[layer] + ratio_ref[layer] * solved[layer + 1]
                        solved[mirror] = field[mirror] + ratio_ref[layer] * solved[mirror - 1]
                parts = []
                for chunk in chunks[number:number + 2]:
                    even, odd = solved[2 * chunk], solved[2 * chunk + 1]
                    upper = jnp.where(low, even, pltpu.roll(odd, BOX, 1))
                    lower = jnp.where(low, pltpu.roll(even, BOX, 1), odd)
                    parts.append(jnp.concatenate([upper, lower], axis=0))
                wide = rows_dot(left, jnp.concatenate(parts, axis=1))
                pieces += [wide[:, :LANES], wide[:, LANES:]]
            potential = lanes_dot(jnp.concatenate(pieces, axis=0), right)
            for number, chunk in enumerate(chunks):
                values = potential[number * BOX:(number + 1) * BOX] * scale
                padded[2, PAD + chunk, HALF:HALF + BOX, :] = values * partner[chunk].astype(F32)

        offset = [jnp.where(is_mine, 0, value) for value in offset]
        flat = BOX * offset[1] + offset[2]
        for place in range(0, CHUNKS, GROUP):
            moved = shifted(padded, 2, range(place, place + GROUP), HALF + offset[0], flat, -offset[2])
            for chunk in range(place, place + GROUP):
                out_ref[:, chunk * LANES:(chunk + 1) * LANES] += moved[chunk]
        return carry

    lax.fori_loop(0, NEAR, pair, 0)

    for slot in range(NEAR):
        source = own if slot < 4 else near.at[2 + slot % 2]
        if slot < 6:
            tab_copy(slot, tab_here).wait_send()
        if slot not in (2, 3, 6, 7):
            box_copy(slot, source).wait_send()

    for holds, slot in ((hands_behind, 6), (core == 0, 7)):
        @pl.when(holds)
        def _():
            tab_copy(slot, tab_here).wait_send()
            box_copy(slot, own).wait_send()

    for holds, copies in ((core == 0, pass_on(7, ahead)), (passes_behind, pass_on(6, behind))):
        @pl.when(holds)
        def _():
            for copy in copies:
                copy.wait_send()

    @pl.when(core == 0)
    def _():
        box_copy(2, own).wait_send()

    @pl.when(core == 1)
    def _():
        box_copy(3, own).wait_send()


def body(orbitals, pair_table):
    left, right, ratios = tables()
    operands = [orbitals.reshape(BOX, BOX * BOX), pair_table.reshape(ROWS, 5)]
    operands += [jnp.asarray(table) for table in (left, right, ratios)]
    cube = (CHUNKS, BOX, LANES)
    dma = pltpu.SemaphoreType.DMA((NEAR + 2,))
    result = pl.pallas_call(
        kernel,
        out_shape=pltpu.VMEM((BOX, BOX * BOX), F32),
        in_specs=[pl.BlockSpec(memory_space=pltpu.HBM)] * 5,
        out_specs=pl.BlockSpec(memory_space=pltpu.VMEM),
        scratch_shapes=[
            pltpu.VMEM((BOX, BOX * BOX), BF16),
            pltpu.VMEM(left.shape, BF16),
            pltpu.VMEM(right.shape, BF16),
            pltpu.VMEM(ratios.shape, F32),
            pltpu.VMEM(cube, BF16),
            pltpu.VMEM((NEAR,) + cube, BF16),
            pltpu.SMEM((ROWS, 5), jnp.int32),
            pltpu.SMEM((NEAR, ROWS, 5), jnp.int32),
            pltpu.VMEM((3, CHUNKS + 2 * PAD, 2 * BOX, LANES), F32),
            pltpu.VMEM(cube, BF16),
            pltpu.VMEM((BOX, HALF, LANES), F32),
            dma, dma, dma, dma,
            pltpu.SemaphoreType.REGULAR((2,)),
            pltpu.SemaphoreType.DMA((5,)),
        ],
        compiler_params=pltpu.CompilerParams(
            collective_id=0, has_side_effects=True, vmem_limit_bytes=32 * 1024 * 1024),
    )(*(pltpu.with_memory_space_constraint(operand, pltpu.HBM) for operand in operands))
    return result.reshape(orbitals.shape)


def solution(mesh):
    in_specs = (P("gx", "gy", None, None, None), P("gx", "gy", None, None))
    out_specs = P("gx", "gy", None, None, None)
    return jax.shard_map(body, mesh=mesh, in_specs=in_specs, out_specs=out_specs, check_vma=False)
```

```python
import math

import jax
import jax.numpy as jnp
import numpy as np
from jax import lax
from jax.experimental import pallas as pl
from jax.experimental.pallas import tpu as pltpu
from jax.sharding import PartitionSpec as P

MESH = pl.DeviceIdType.MESH
F32 = jnp.float32
BF16 = jnp.bfloat16
BOX = 64
HALF = BOX // 2
LANES = 128
CHUNKS = BOX * BOX // LANES
PAD = 17
ROWS = 4
NEAR = 8
GROUP = 32


def tables():
    cells = np.arange(BOX, dtype=np.float64) + 1
    sine = np.sin(math.pi * cells[:, None] * cells[None, :] / (BOX + 1))
    high = sine.astype(BF16)
    low = (sine - high.astype(np.float64)).astype(BF16)
    none = np.zeros_like(high)
    both = lambda part: np.block([[part, none], [none, part]])
    left = np.block([[high, high], [low, none]])
    right = np.block([[both(high), both(low)], [both(high), both(none)]])
    eigen = 2 - 2 * np.cos(math.pi * cells / (BOX + 1))
    row = np.arange(HALF)[:, None]
    lane = np.arange(LANES)[None, :]
    middle = 2 + eigen[lane // BOX * HALF + row] + eigen[lane % BOX]
    ratios = [1 / middle]
    for _ in range(HALF - 1):
        ratios.append(1 / (middle - ratios[-1]))
    ratios.append(1 / (1 - ratios[-1] ** 2))
    return left, right, np.stack(ratios).astype(np.float32)


def split(values):
    high = values.astype(BF16)
    return high, (values - high.astype(F32)).astype(BF16)


def rows_dot(left, values):
    high, low = split(values)
    both = jnp.dot(left, jnp.concatenate([high, low], axis=0), preferred_element_type=F32)
    return both[:BOX] + both[BOX:]


def lanes_dot(values, right):
    high, low = split(values)
    both = jnp.dot(jnp.concatenate([high, low], axis=1), right, preferred_element_type=F32)
    return both[:, :LANES] + both[:, LANES:]


def shift_masks(amount, offset):
    lane = lax.broadcasted_iota(jnp.int32, (BOX, LANES), 1)
    cell = (lane & (BOX - 1)) - offset
    inside = (cell >= 0) & (cell < BOX)
    return (lane < LANES - amount) & inside, (lane >= LANES - amount) & inside


def shifted(source, slot, chunks, row, flat, offset):
    start, amount = PAD + (flat >> 7), flat & (LANES - 1)
    here, after = shift_masks(amount, offset)
    turned = {}

    def turn(chunk):
        if chunk not in turned:
            values = source[slot, start + chunk, pl.ds(row, BOX), :]
            turned[chunk] = pltpu.roll(values, LANES - amount, 1)
        return turned[chunk]

    return {chunk: jnp.where(here, turn(chunk), jnp.where(after, turn(chunk + 1), 0.0)) for chunk in chunks}


def kernel(
    orb_hbm, tab_hbm, left_hbm, right_hbm, ratio_hbm, out_ref,
    orb_ref, left_ref, right_ref, ratio_ref,
    own, near, tab_here, tab_near, padded, partner, field,
    box_send, box_recv, tab_send, tab_recv, ready, local_sem,
):
    span_x, span_y = lax.axis_size("gx"), lax.axis_size("gy")
    here_x, here_y = lax.axis_index("gx"), lax.axis_index("gy")
    core = lax.rem(here_y, 2)
    sign = 1 - 2 * core

    def at(step_x, step_y):
        return (lax.rem(here_x + step_x + span_x, span_x), lax.rem(here_y + step_y + span_y, span_y))

    twin, beyond, ahead, behind = at(0, sign), at(0, -sign), at(1, 0), at(-1, 0)
    owners = [twin, beyond, ahead, behind, at(1, sign), at(-1, sign), at(1, -sign), at(-1, -sign)]
    dests = [twin, beyond, behind, ahead, twin, twin, beyond, beyond]

    def by_step(step, order):
        slot = order[0]
        for number in range(1, NEAR):
            slot = jnp.where(step == number, order[number], slot)
        return slot

    def pick(slot):
        chosen = owners[0]
        for number in range(1, NEAR):
            chosen = tuple(jnp.where(slot == number, new, old) for new, old in zip(owners[number], chosen))
        return chosen

    barrier = pltpu.get_barrier_semaphore()
    for device in (ahead, behind):
        pl.semaphore_signal(barrier, inc=1, device_id=device, device_id_type=MESH)
    for signals, device in ((core == 1, twin), (here_y < span_y - 1, beyond)):
        @pl.when(signals)
        def _():
            pl.semaphore_signal(barrier, inc=1, device_id=device, device_id_type=MESH)

    loads = [
        pltpu.make_async_copy(source, dest, local_sem.at[number])
        for number, (source, dest) in enumerate((
            (orb_hbm, orb_ref), (tab_hbm, tab_here), (left_hbm, left_ref), (right_hbm, right_ref), (ratio_hbm, ratio_ref)))
    ]
    for load in loads:
        load.start()
    loads[0].wait()
    for chunk in range(CHUNKS):
        own[chunk] = orb_ref[:, chunk * LANES:(chunk + 1) * LANES]
    loads[1].wait()
    pl.semaphore_wait(barrier, 2 + jnp.where(core == 0, 1, 0) + jnp.where(here_y == 0, 0, 1))
    for answers, device, number in ((core == 0, twin, 0), (here_y == span_y - 1, beyond, 1)):
        @pl.when(answers)
        def _():
            pl.semaphore_signal(ready.at[number], inc=1, device_id=device, device_id_type=MESH)

    def box_copy(slot, source):
        return pltpu.make_async_remote_copy(
            src_ref=source, dst_ref=near.at[slot], send_sem=box_send.at[slot],
            recv_sem=box_recv.at[slot], device_id=dests[slot] if isinstance(slot, int) else twin, device_id_type=MESH)

    def tab_copy(slot, source):
        return pltpu.make_async_remote_copy(
            src_ref=source, dst_ref=tab_near.at[slot], send_sem=tab_send.at[slot],
            recv_sem=tab_recv.at[slot], device_id=dests[slot] if isinstance(slot, int) else twin, device_id_type=MESH)

    def send_own(slot):
        tab_copy(slot, tab_here).start()
        box_copy(slot, own).start()

    def hand_on(slot, source):
        tab_copy(slot, tab_near.at[source]).start()
        box_copy(slot, near.at[source]).start()

    def pass_on(slot, device):
        return [
            pltpu.make_async_remote_copy(
                src_ref=here.at[1], dst_ref=here.at[slot], send_sem=send.at[NEAR + slot - 6],
                recv_sem=recv.at[slot], device_id=device, device_id_type=MESH)
            for here, send, recv in ((tab_near, tab_send, tab_recv), (near, box_send, box_recv))
        ]

    twin_last = (here_x == 0) & (here_y == 1)

    def send_twin():
        pl.semaphore_wait(ready.at[0], 1)
        send_own(0)

    @pl.when(here_y > 0)
    def _():
        send_own(1)

    @pl.when(core == 0)
    def _():
        send_own(3)
        send_own(0)

    @pl.when(core == 1)
    def _():
        send_own(2)

    padded[...] = jnp.zeros_like(padded)
    out_ref[...] = jnp.zeros_like(out_ref)
    padded[0, PAD:PAD + CHUNKS, HALF:HALF + BOX, :] = own[...].astype(F32)

    @pl.when((core == 1) & jnp.logical_not(twin_last))
    def _():
        send_twin()

    for load in loads[2:]:
        load.wait()

    hands_behind = ((core == 1) & (here_y < span_y - 1)) | (here_y == 2)
    passes_behind = ((core == 1) & (here_y != 1)) | (here_y == 0)
    left, right = left_ref[...], right_ref[...]
    low = lax.broadcasted_iota(jnp.int32, (HALF, LANES), 1) < BOX
    me = here_x * span_y + here_y

    def pair(step, carry):
        on_first = jnp.where(here_y == 0, jnp.where(here_x == span_x - 1, by_step(step, (0, 3, 4, 1, 2, 5, 7, 6)), by_step(step, (0, 3, 4, 1, 2, 5, 6, 7))), by_step(step, (0, 3, 1, 4, 2, 6, 5, 7)))
        on_second = jnp.where(twin_last, by_step(step, (2, 1, 0, 5, 3, 7, 4, 6)), by_step(step, (0, 2, 5, 1, 3, 7, 4, 6)))
        slot = jnp.where(core == 0, on_first, on_second)
        owner = pick(slot)
        other = owner[0] * span_y + owner[1]

        @pl.when((step == 1) & (core == 0))
        def _():
            box_copy(3, own).wait_send()
            send_own(2)

        @pl.when((step == 1) & (core == 1))
        def _():
            box_copy(2, own).wait_send()
            send_own(3)

        @pl.when((step == 1) & (here_y == 0))
        def _():
            pl.semaphore_wait(ready.at[1], 1)
            send_own(1)

        tab_copy(slot, tab_here).wait_recv()
        box_copy(slot, own).wait_recv()

        @pl.when((slot == 2) & twin_last)
        def _():
            send_twin()

        @pl.when((slot == 2) & hands_behind)
        def _():
            hand_on(6, 2)

        @pl.when((slot == 3) & (core == 0))
        def _():
            hand_on(7, 3)

        for first_hop, inward in ((2, 4), (3, 5)):
            @pl.when(slot == first_hop)
            def _():
                hand_on(inward, first_hop)

        @pl.when((slot == 1) & (core == 0))
        def _():
            for copy in pass_on(7, ahead):
                copy.start()

        @pl.when((slot == 1) & passes_behind)
        def _():
            for copy in pass_on(6, behind):
                copy.start()

        listed = jnp.int32(0)
        wanted = jnp.int32(0)
        offset = [jnp.int32(0)] * 3
        for row in range(ROWS):
            mine = (tab_here[row, 0] == me) & (tab_here[row, 1] == other)
            theirs = (tab_near[slot, row, 0] == other) & (tab_near[slot, row, 1] == me)
            listed = jnp.where(mine, 1, listed)
            wanted = jnp.where(theirs, 1, wanted)
            for dim in range(3):
                value = jnp.where(theirs, tab_near[slot, row, 2 + dim], offset[dim])
                offset[dim] = jnp.where(mine, tab_here[row, 2 + dim], value)
        is_mine = listed == 1
        scale = jnp.where(listed + wanted > 0, -((2 / (BOX + 1)) ** 2), 0.0)
        second = listed
        first = 1 - listed
        padded[1, PAD:PAD + CHUNKS, HALF:HALF + BOX, :] = near[slot].astype(F32)

        flat = -(BOX * offset[1] + offset[2])
        order = [chunk for number in range(CHUNKS // 2) for chunk in (number, CHUNKS - 1 - number)]
        front = back = None
        for place in range(0, CHUNKS, GROUP):
            chunks = order[place:place + GROUP]
            moved = shifted(padded, second, sorted(chunks), HALF - offset[0], flat, offset[2])
            products = []
            for chunk in chunks:
                fixed = padded[first, PAD + chunk, HALF:HALF + BOX, :]
                products.append(moved[chunk] * fixed)
                partner[chunk] = jnp.where(is_mine, moved[chunk], fixed).astype(BF16)
            along = lanes_dot(jnp.concatenate(products, axis=0), right)
            for number in range(0, GROUP, 2):
                begin = number * BOX
                wide = jnp.concatenate([along[begin:begin + BOX], along[begin + BOX:begin + 2 * BOX]], axis=1)
                wide = rows_dot(left, wide)
                layers = []
                for part in range(2):
                    upper = wide[:HALF, part * LANES:(part + 1) * LANES]
                    lower = wide[HALF:, part * LANES:(part + 1) * LANES]
                    layers.append(jnp.where(low, upper, pltpu.roll(lower, BOX, 1)))
                    layers.append(jnp.where(low, pltpu.roll(upper, BOX, 1), lower))
                for layer, one, two in ((0, layers[0], layers[3]), (1, layers[1], layers[2])):
                    layer += 2 * chunks[number]
                    if layer > 0:
                        one, two = one + front, two + back
                    front, back = one * ratio_ref[layer], two * ratio_ref[layer]
                    field[layer] = front
                    field[BOX - 1 - layer] = back

        last, closing = ratio_ref[HALF - 1], ratio_ref[HALF]
        solved = {HALF - 1: (front + last * back) * closing, HALF: (back + last * front) * closing}
        order = [chunk for number in reversed(range(CHUNKS // 2)) for chunk in (number, CHUNKS - 1 - number)]
        for place in range(0, CHUNKS, GROUP):
            chunks = order[place:place + GROUP]
            pieces = []
            for number in range(0, GROUP, 2):
                for layer in (2 * chunks[number] + 1, 2 * chunks[number]):
                    if layer < HALF - 1:
                        mirror = BOX - 1 - layer
                        solved[layer] = field[layer] + ratio_ref[layer] * solved[layer + 1]
                        solved[mirror] = field[mirror] + ratio_ref[layer] * solved[mirror - 1]
                parts = []
                for chunk in chunks[number:number + 2]:
                    even, odd = solved[2 * chunk], solved[2 * chunk + 1]
                    upper = jnp.where(low, even, pltpu.roll(odd, BOX, 1))
                    lower = jnp.where(low, pltpu.roll(even, BOX, 1), odd)
                    parts.append(jnp.concatenate([upper, lower], axis=0))
                wide = rows_dot(left, jnp.concatenate(parts, axis=1))
                pieces += [wide[:, :LANES], wide[:, LANES:]]
            potential = lanes_dot(jnp.concatenate(pieces, axis=0), right)
            for number, chunk in enumerate(chunks):
                values = potential[number * BOX:(number + 1) * BOX] * scale
                padded[2, PAD + chunk, HALF:HALF + BOX, :] = values * partner[chunk].astype(F32)

        offset = [jnp.where(is_mine, 0, value) for value in offset]
        flat = BOX * offset[1] + offset[2]
        for place in range(0, CHUNKS, GROUP):
            moved = shifted(padded, 2, range(place, place + GROUP), HALF + offset[0], flat, -offset[2])
            for chunk in range(place, place + GROUP):
                out_ref[:, chunk * LANES:(chunk + 1) * LANES] += moved[chunk]
        return carry

    lax.fori_loop(0, NEAR, pair, 0)

    for slot in range(NEAR):
        source = own if slot < 4 else near.at[2 + slot % 2]
        if slot < 6:
            tab_copy(slot, tab_here).wait_send()
        if slot not in (2, 3, 6, 7):
            box_copy(slot, source).wait_send()

    for holds, slot in ((hands_behind, 6), (core == 0, 7)):
        @pl.when(holds)
        def _():
            tab_copy(slot, tab_here).wait_send()
            box_copy(slot, own).wait_send()

    for holds, copies in ((core == 0, pass_on(7, ahead)), (passes_behind, pass_on(6, behind))):
        @pl.when(holds)
        def _():
            for copy in copies:
                copy.wait_send()

    @pl.when(core == 0)
    def _():
        box_copy(2, own).wait_send()

    @pl.when(core == 1)
    def _():
        box_copy(3, own).wait_send()


def body(orbitals, pair_table):
    left, right, ratios = tables()
    operands = [orbitals.reshape(BOX, BOX * BOX), pair_table.reshape(ROWS, 5)]
    operands += [jnp.asarray(table) for table in (left, right, ratios)]
    cube = (CHUNKS, BOX, LANES)
    dma = pltpu.SemaphoreType.DMA((NEAR + 2,))
    result = pl.pallas_call(
        kernel,
        out_shape=pltpu.VMEM((BOX, BOX * BOX), F32),
        in_specs=[pl.BlockSpec(memory_space=pltpu.HBM)] * 5,
        out_specs=pl.BlockSpec(memory_space=pltpu.VMEM),
        scratch_shapes=[
            pltpu.VMEM((BOX, BOX * BOX), BF16),
            pltpu.VMEM(left.shape, BF16),
            pltpu.VMEM(right.shape, BF16),
            pltpu.VMEM(ratios.shape, F32),
            pltpu.VMEM(cube, BF16),
            pltpu.VMEM((NEAR,) + cube, BF16),
            pltpu.SMEM((ROWS, 5), jnp.int32),
            pltpu.SMEM((NEAR, ROWS, 5), jnp.int32),
            pltpu.VMEM((3, CHUNKS + 2 * PAD, 2 * BOX, LANES), F32),
            pltpu.VMEM(cube, BF16),
            pltpu.VMEM((BOX, HALF, LANES), F32),
            dma, dma, dma, dma,
            pltpu.SemaphoreType.REGULAR((2,)),
            pltpu.SemaphoreType.DMA((5,)),
        ],
        compiler_params=pltpu.CompilerParams(
            collective_id=0, has_side_effects=True, vmem_limit_bytes=32 * 1024 * 1024),
    )(*(pltpu.with_memory_space_constraint(operand, pltpu.HBM) for operand in operands))
    return result.reshape(orbitals.shape)


def solution(mesh):
    in_specs = (P("gx", "gy", None, None, None), P("gx", "gy", None, None))
    out_specs = P("gx", "gy", None, None, None)
    return jax.shard_map(body, mesh=mesh, in_specs=in_specs, out_specs=out_specs, check_vma=False)
```
